32 devices in a mesh: dp: 16 (over z, x, core), tensor: 2 (over y).
Axes of the slice: x: 2, y: 2, z: 4, core: 2. Of those that a mesh axis runs over, the one named last changes fastest.
Arguments:
- tokens: bfloat16 [4096, 768], P(('dp', 'tensor')), may hold values from -6 to 6
- ln1_gain: bfloat16 [768], P('dp'), may hold values from 0.099609375 to 1.8984375
- ln1_bias: bfloat16 [768], P('dp'), may hold values from -1.5 to 1.5
- ln2_gain: bfloat16 [768], P('dp'), may hold values from 0.099609375 to 1.8984375
- ln2_bias: bfloat16 [768], P('dp'), may hold values from -1.5 to 1.5
- w_qkv: bfloat16 [768, 2304], P('dp', 'tensor'), may hold values from -0.21875 to 0.21875
- w_out: bfloat16 [768, 768], P('tensor', 'dp'), may hold values from -0.875 to 0.875
- w_up: bfloat16 [768, 3072], P('dp', 'tensor'), may hold values from -0.21875 to 0.21875
- w_down: bfloat16 [3072, 768], P('tensor', 'dp'), may hold values from -0.109375 to 0.109375
- grad_out: bfloat16 [4096, 768], P(('dp', 'tensor')), may hold values from -6 to 6
- lengths: int32 [16, 4], P('dp'), may hold values from 1 to 192, 256 in all within a row
Outputs:
- output: bfloat16 [4096, 768], P(('dp', 'tensor'))
- grad_tokens: float32 [4096, 768], P(('dp', 'tensor'))
- grad_ln1_gain: float32 [768], P('dp')
- grad_ln1_bias: float32 [768], P('dp')
- grad_ln2_gain: float32 [768], P('dp')
- grad_ln2_bias: float32 [768], P('dp')
- grad_w_qkv: float32 [768, 2304], P('dp', 'tensor')
- grad_w_out: float32 [768, 768], P('tensor', 'dp')
- grad_w_up: float32 [768, 3072], P('dp', 'tensor')
- grad_w_down: float32 [3072, 768], P('tensor', 'dp')
The draws below stay inside these ranges and needn't reach their ends.
Inputs may be any that keep to these rules, and one draw needn't show every extreme that they name: Each row of lengths gives, in order, the lengths of the 4 sequences packed into the 256 tokens of one group; a row sums to 256 and its longest sequence has exactly 192 tokens.
All inputs are finite; a program needn't handle non-finite values.
Results may differ from the reference program's by a relative error of at most 0.0099.
Values may be sent and summed in bfloat16 or wider, within the bound.
A program may use at most 128 MiB of HBM per device.

```python
import math
import jax
import jax.numpy as jnp
import numpy as np
from jax import lax

D = 768
HEADS = 12
HEAD = 64
ROT = 16
FF = 3072
SEQS = 4
GROUP = 256
LONGEST = 192
TOKENS = 4096
N_DP = 16


def strengthened(values, stream_key, source, target, parts, factor):
    owner, partner = [(jnp.arange(values.shape[axis_at]) // (values.shape[axis_at] // parts)).reshape([-1 if axis == axis_at else 1 for axis in range(values.ndim)]) for axis_at in (source, target)]
    chosen = jax.random.permutation(stream_key, parts)[partner]
    strong = (owner == chosen) | (owner == (partner + parts // 2) % parts)
    return jnp.where(strong, factor * values, values)


def block_scale(key, extent, pieces, least, largest):
    def one(dim, blocks):
        steps = jax.random.uniform(jax.random.fold_in(jax.random.fold_in(key, 6), dim), (blocks,), jnp.float32, least / len(pieces), largest / len(pieces))
        return jnp.repeat(jnp.exp(steps), extent[dim] // blocks).reshape((-1,) + (1,) * (len(extent) - dim - 1))

    factor_of = one(*pieces[0])
    for cut in pieces[1:]:
        factor_of = factor_of * one(*cut)
    return factor_of


def length_profile(number_of, total, limit, slope):
    loads = [(1 << 20) // math.isqrt(standing ** slope) + 1 for standing in range(2, number_of + 1)]
    spare, counts = total - limit - (number_of - 1), [1] * (number_of - 1)
    while spare > 0:
        movable = [i for i in range(number_of - 1) if counts[i] < limit]
        mass, budget = sum([loads[i] for i in movable]), spare
        for i in movable:
            addition = min(limit - counts[i], max(1, budget * loads[i] // mass), spare)
            counts[i] = counts[i] + addition
            spare = spare - addition
    return np.array([limit] + counts)


def uneven(key, number_of, total, limit, lean):
    if number_of == 2:
        one = jax.random.randint(key, (), max(1, total - limit), min(limit, total - 1) + 1)
        return jnp.stack([one, total - one])
    sizes = jnp.asarray(length_profile(number_of, total, limit, lean), jnp.int32)
    twos = (number_of - 1) // 2
    giver, sink = sizes[1:1 + 2 * twos:2], sizes[2:2 + 2 * twos:2]
    margin = jnp.minimum(giver - 1, limit - sink)
    shifted = jax.random.randint(jax.random.fold_in(key, 1), (twos,), 0, 1 << 20) % (margin + 1)
    sizes = sizes.at[1:1 + 2 * twos:2].set(giver - shifted).at[2:2 + 2 * twos:2].set(sink + shifted)
    return sizes[jax.random.permutation(jax.random.fold_in(key, 2), number_of)]


def noise(rng, shape, deviation, bound, shards=(), held_as=jnp.bfloat16):
    drawn = jax.random.normal(rng, shape, jnp.float32) * deviation
    if len(shards) > 0:
        drawn = block_scale(rng, shape, shards, -0.22, 0.18) * drawn
    return jnp.clip(drawn, min=-bound, max=bound).astype(held_as)


def gaussian_with(own_key, shape, deviation, bound, split, heavy, kind=jnp.bfloat16):
    values = deviation * jax.random.normal(own_key, shape, jnp.float32)
    if split:
        values = values * block_scale(own_key, shape, split, -0.22, 0.18)
    return jnp.clip(strengthened(values, jax.random.fold_in(own_key, 3), *heavy), -bound, bound).astype(kind)


def setup_inputs(seed: int = 0) -> dict:
    streams_of = jax.random.split(jax.random.key(seed), 12)
    return {
        "tokens": gaussian_with(streams_of[0], (TOKENS, D), 1.0, 6.0, ((0, 32),), (0, 1, 32, 2.75)),
        "ln1_gain": jnp.clip(1.0 + 0.18 * jax.random.normal(streams_of[1], (D,), jnp.float32), 0.099609375, 1.8984375).astype(jnp.bfloat16),
        "ln1_bias": noise(streams_of[2], (D,), 0.3, 1.5, ((0, 16),)),
        "ln2_gain": jnp.clip(1.0 + 0.18 * jax.random.normal(streams_of[3], (D,), jnp.float32), 0.099609375, 1.8984375).astype(jnp.bfloat16),
        "ln2_bias": noise(streams_of[4], (D,), 0.3, 1.5, ((0, 16),)),
        "w_qkv": noise(streams_of[5], (D, 3 * D), D ** -0.5, 0.21875, ((0, 16), (1, 2))),
        "w_out": noise(streams_of[6], (D, D), (D // 16) ** -0.5, 0.875, ((0, 2), (1, 16))),
        "w_up": noise(streams_of[7], (D, FF), D ** -0.5, 0.21875, ((0, 16), (1, 2))),
        "w_down": noise(streams_of[8], (FF, D), FF ** -0.5, 0.109375, ((0, 2), (1, 16))),
        "grad_out": gaussian_with(streams_of[9], (TOKENS, D), 1.0, 6.0, ((0, 32),), (0, 1, 32, 2.75)),
        "lengths": jax.vmap(lambda own: uneven(own, SEQS, GROUP, LONGEST, 2))(jax.random.split(streams_of[10], N_DP)).reshape((N_DP, SEQS)).astype(jnp.int32),
    }


@jax.custom_vjp
def low(v):
    return lax.optimization_barrier(v.astype(jnp.bfloat16)).astype(jnp.float32)

@jax.custom_vjp
def low_back(v):
    return v

def low_keep(v):
    return (low(v), None)

def low_pass(kept, grad):
    return (grad,)

def back_keep(v):
    return (v, None)

def back_low(kept, grad):
    return (low(grad),)
low.defvjp(low_keep, low_pass)
low_back.defvjp(back_keep, back_low)
norm_eps = 1e-05
masked_score = -1e+30
highest = lax.Precision.HIGHEST

def layer_norm(values, norm_gain, norm_bias):
    center = values - lax.optimization_barrier(jnp.mean(values, axis=-1, keepdims=True))
    spread = lax.optimization_barrier(jnp.mean(center * center, axis=-1, keepdims=True))
    return center * lax.rsqrt(spread + norm_eps) * norm_gain + norm_bias

def doc_layout(lengths_row, row_count):
    seq_ends = jnp.cumsum(lengths_row).astype(jnp.int32)
    starts = (seq_ends - lengths_row).astype(jnp.int32)
    places = jnp.arange(row_count, dtype=jnp.int32)
    segment = lax.optimization_barrier(jnp.sum((places[:, None] >= seq_ends[None, :]).astype(jnp.int32), axis=1)).astype(jnp.int32)
    chosen = segment[:, None] == jnp.arange(lengths_row.shape[0], dtype=jnp.int32)[None, :]
    seq_first = lax.optimization_barrier(jnp.sum(jnp.where(chosen, starts[None, :], 0), axis=1)).astype(jnp.int32)
    return (segment, (places - seq_first).astype(jnp.int32), places)

def rope_tables(positions):
    frequency = jnp.arange(ROT // 2, dtype=jnp.float32)
    inverse = jnp.exp(frequency * (-2.0 * math.log(10000.0) / ROT))
    angles = positions.astype(jnp.float32)[:, None] * inverse[None, :]
    return (jnp.cos(angles), jnp.sin(angles))

def rotate(vectors, wave_cos, wave_sin):
    half_rot = ROT // 2
    first_half = vectors[..., :half_rot]
    second_half = vectors[..., half_rot:ROT]
    cos_heads = wave_cos[:, None, :]
    sin_heads = wave_sin[:, None, :]
    return jnp.concatenate([first_half * cos_heads - second_half * sin_heads, second_half * cos_heads + first_half * sin_heads, vectors[..., ROT:]], axis=-1)

def block_layer(tokens_f, params, lengths_row):
    gain_one, bias_one, gain_two, bias_two, qkv_weight, out_weight, up_weight, down_weight = params
    row_count = tokens_f.shape[0]
    segment, positions, places = doc_layout(lengths_row, row_count)
    allowed = (segment[:, None] == segment[None, :]) & (places[:, None] >= places[None, :])
    wave_cos, wave_sin = rope_tables(positions)
    normed_one = low(layer_norm(tokens_f, gain_one, bias_one))
    normed_two = low(layer_norm(tokens_f, gain_two, bias_two))
    projected = low_back(jnp.dot(normed_one, qkv_weight, precision=highest)).reshape(row_count, HEADS, 3, HEAD)
    queries = low(rotate(projected[:, :, 0], wave_cos, wave_sin))
    keys_all = low(rotate(projected[:, :, 1], wave_cos, wave_sin))
    values_all = low(projected[:, :, 2])
    scores = low_back(jnp.einsum('qhd,khd->hqk', queries, keys_all, precision=highest) * (1.0 / math.sqrt(HEAD)))
    scores = jnp.where(allowed[None], scores, masked_score)
    row_peak = lax.optimization_barrier(jnp.max(scores, axis=-1, keepdims=True))
    exponent = jnp.exp(scores - row_peak)
    probability = exponent / lax.optimization_barrier(jnp.sum(exponent, axis=-1, keepdims=True))
    attended = jnp.einsum('hqk,khd->qhd', low(probability), values_all, precision=highest)
    attended = low(low_back(attended)).reshape(row_count, HEADS * HEAD)
    hidden_pre = low_back(jnp.dot(normed_two, up_weight, precision=highest))
    activated = low(jax.nn.gelu(hidden_pre, approximate=False))
    branches = jnp.dot(attended, out_weight, precision=highest) + jnp.dot(activated, down_weight, precision=highest)
    return tokens_f + branches

def reference(tokens, ln1_gain, ln1_bias, ln2_gain, ln2_bias, w_qkv, w_out, w_up, w_down, grad_out, lengths):
    params = tuple((element.astype(jnp.float32) for element in (ln1_gain, ln1_bias, ln2_gain, ln2_bias, w_qkv, w_out, w_up, w_down)))
    group_rows = tokens.shape[0] // N_DP
    tokens_groups = tokens.astype(jnp.float32).reshape(N_DP, group_rows, tokens.shape[1])
    grad_groups = grad_out.astype(jnp.float32).reshape(N_DP, group_rows, tokens.shape[1])

    def one_group(totals, inputs_now):
        tokens_now, cotangent, lengths_now = inputs_now

        def forward(tokens_arg, *param_args):
            return block_layer(tokens_arg, param_args, lengths_now)
        result, pullback = jax.vjp(forward, tokens_now, *params)
        pulled = pullback(cotangent)
        totals = tuple((running + addend for running, addend in zip(totals, pulled[1:])))
        return (totals, (result, pulled[0]))
    start_totals = tuple((jnp.zeros_like(element) for element in params))
    totals, (results, input_grads) = lax.scan(one_group, start_totals, (tokens_groups, grad_groups, lengths))
    output = results.reshape(tokens.shape).astype(jnp.bfloat16)
    grad_tokens = input_grads.reshape(tokens.shape)
    return (output, grad_tokens, totals[0], totals[1], totals[2], totals[3], totals[4], totals[5], totals[6], totals[7])
```

```python
import math

import jax
import jax.numpy as jnp
from jax import lax
from jax.experimental import pallas as pl
from jax.experimental.pallas import tpu as pltpu
from jax.sharding import PartitionSpec as P

HEAD = 64
ROT = 16


norm_eps = 1e-05
masked_score = -1e30


def layer_norm(values, norm_gain, norm_bias):
    center = values - jnp.mean(values, axis=-1, keepdims=True)
    spread = jnp.mean(center * center, axis=-1, keepdims=True)
    return center * lax.rsqrt(spread + norm_eps) * norm_gain + norm_bias


def norms_pair(rows_f, gain_one, bias_one, gain_two, bias_two):
    return (layer_norm(rows_f, gain_one, bias_one), layer_norm(rows_f, gain_two, bias_two))


def doc_layout(lengths_row, row_count):
    seq_ends = jnp.cumsum(lengths_row)
    starts = seq_ends - lengths_row
    places = jnp.arange(row_count, dtype=jnp.int32)
    segment = jnp.sum((places[:, None] >= seq_ends[None, :]).astype(jnp.int32), axis=1)
    chosen = segment[:, None] == jnp.arange(lengths_row.shape[0], dtype=jnp.int32)[None, :]
    seq_first = jnp.sum(jnp.where(chosen, starts[None, :], 0), axis=1)
    return (segment, places - seq_first, places)


def rope_tables(positions):
    frequency = jnp.arange(ROT // 2, dtype=jnp.float32)
    inverse = jnp.exp(frequency * (-2.0 * math.log(10000.0) / ROT))
    angles = positions.astype(jnp.float32)[:, None] * inverse[None, :]
    return (jnp.cos(angles), jnp.sin(angles))


def rotate(vectors, wave_cos, wave_sin):
    half_rot = ROT // 2
    first_half = vectors[..., :half_rot]
    second_half = vectors[..., half_rot:ROT]
    cos_heads = wave_cos[:, None, :]
    sin_heads = wave_sin[:, None, :]
    return jnp.concatenate(
        [
            first_half * cos_heads - second_half * sin_heads,
            second_half * cos_heads + first_half * sin_heads,
            vectors[..., ROT:],
        ],
        axis=-1,
    )


def contract(first_op, second_op, first_dim, second_dim):
    return lax.dot_general(
        first_op,
        second_op,
        (((first_dim,), (second_dim,)), ((), ())),
        preferred_element_type=jnp.float32,
    )


def per_device(
    tokens, ln1_gain, ln1_bias, ln2_gain, ln2_bias, w_qkv, w_out, w_up, w_down, grad_out, lengths
):
    tok_rows = tokens.shape[0]
    group_rows = tok_rows * lax.axis_size("tensor")
    local_heads = w_qkv.shape[1] // (3 * HEAD)
    score_scale = 1.0 / math.sqrt(HEAD)
    norm_params = jnp.stack([ln1_gain, ln1_bias, ln2_gain, ln2_bias], axis=0)
    qkv_full, up_full, out_full, down_full, norm_full = (
        lax.all_gather(w_qkv, "dp", axis=0, tiled=True),
        lax.all_gather(w_up, "dp", axis=0, tiled=True),
        lax.all_gather(w_out, "dp", axis=1, tiled=True),
        lax.all_gather(w_down, "dp", axis=1, tiled=True),
        lax.all_gather(norm_params, "dp", axis=1, tiled=True),
    )
    norm_float = norm_full.astype(jnp.float32)
    gain_one, bias_one, gain_two, bias_two = (
        norm_float[0],
        norm_float[1],
        norm_float[2],
        norm_float[3],
    )
    segment, positions, places = doc_layout(lengths[0], group_rows)
    wave_cos, wave_sin = rope_tables(positions)
    tokens_f = tokens.astype(jnp.float32)
    own_one, own_two = norms_pair(tokens_f, gain_one, bias_one, gain_two, bias_two)
    normed_one, normed_two = (
        lax.all_gather(own_one.astype(jnp.bfloat16), "tensor", axis=0, tiled=True),
        lax.all_gather(own_two.astype(jnp.bfloat16), "tensor", axis=0, tiled=True),
    )
    projected = jnp.dot(normed_one, qkv_full, preferred_element_type=jnp.float32).reshape(
        group_rows, local_heads, 3, HEAD
    )
    queries = rotate(projected[:, :, 0], wave_cos, wave_sin).astype(jnp.bfloat16)
    keys_all = rotate(projected[:, :, 1], wave_cos, wave_sin).astype(jnp.bfloat16)
    values_all = projected[:, :, 2].astype(jnp.bfloat16)
    block_rows = min(512, group_rows)
    block_count = group_rows // block_rows
    query_blocks = queries.reshape(block_count, block_rows, local_heads, HEAD)
    segment_blocks = segment.reshape(block_count, block_rows)
    place_blocks = places.reshape(block_count, block_rows)

    def block_scores(query_block, segment_block, place_block):
        scores = (
            jnp.einsum("qhd,khd->hqk", query_block, keys_all, preferred_element_type=jnp.float32)
            * score_scale
        )
        allowed = (segment_block[:, None] == segment[None, :]) & (
            place_block[:, None] >= places[None, :]
        )
        return jnp.where(allowed[None], scores, masked_score)

    def attend_block(block_items):
        query_block, segment_block, place_block = block_items
        scores = block_scores(query_block, segment_block, place_block)
        row_peak = jnp.max(scores, axis=-1, keepdims=True)
        exponent = jnp.exp(scores - row_peak)
        row_total = jnp.sum(exponent, axis=-1, keepdims=True)
        prob_low = (exponent / row_total).astype(jnp.bfloat16)
        attended_block = jnp.einsum(
            "hqk,khd->qhd", prob_low, values_all, preferred_element_type=jnp.float32
        )
        return (attended_block.astype(jnp.bfloat16), row_peak + jnp.log(row_total))

    attended_blocks, log_totals = lax.map(
        attend_block, (query_blocks, segment_blocks, place_blocks)
    )
    attended = attended_blocks.reshape(group_rows, local_heads * HEAD)
    hidden_pre = jnp.dot(normed_two, up_full, preferred_element_type=jnp.float32)
    activated = jax.nn.gelu(hidden_pre, approximate=False).astype(jnp.bfloat16)
    branch_terms = jnp.dot(attended, out_full, preferred_element_type=jnp.float32) + jnp.dot(
        activated, down_full, preferred_element_type=jnp.float32
    )
    branch_own = lax.psum_scatter(branch_terms, "tensor", scatter_dimension=0, tiled=True)
    output = (tokens_f + branch_own).astype(jnp.bfloat16)
    cotangent = lax.all_gather(grad_out, "tensor", axis=0, tiled=True)
    qkv_back, up_back, out_back, down_back = (
        lax.all_gather(w_qkv, "dp", axis=0, tiled=True),
        lax.all_gather(w_up, "dp", axis=0, tiled=True),
        lax.all_gather(w_out, "dp", axis=1, tiled=True),
        lax.all_gather(w_down, "dp", axis=1, tiled=True),
    )
    act_grad = contract(cotangent, down_back, 1, 1)
    gelu_value, gelu_pull = jax.vjp(
        lambda pre_act: jax.nn.gelu(pre_act, approximate=False), hidden_pre
    )
    pre_grad = gelu_pull(act_grad)[0].astype(jnp.bfloat16)
    grad_down_t = contract(cotangent, activated, 0, 0)
    grad_up = contract(normed_two, pre_grad, 0, 0)
    norm_two_grad = contract(pre_grad, up_back, 1, 1)
    att_grad = contract(cotangent, out_back, 1, 1).astype(jnp.bfloat16)
    grad_out_t = contract(cotangent, attended, 0, 0)
    att_blocks = att_grad.reshape(block_count, block_rows, local_heads, HEAD)

    def back_block(carry, block_items):
        key_grads, value_grads = carry
        query_block, segment_block, place_block, grad_block, log_block = block_items
        scores = block_scores(query_block, segment_block, place_block)
        probability = jnp.exp(scores - log_block)
        prob_grad = jnp.einsum(
            "qhd,khd->hqk", grad_block, values_all, preferred_element_type=jnp.float32
        )
        row_dot = jnp.sum(probability * prob_grad, axis=-1, keepdims=True)
        score_grad = (probability * (prob_grad - row_dot)).astype(jnp.bfloat16)
        query_grad = (
            jnp.einsum("hqk,khd->qhd", score_grad, keys_all, preferred_element_type=jnp.float32)
            * score_scale
        )
        key_grads = (
            key_grads
            + jnp.einsum(
                "hqk,qhd->khd", score_grad, query_block, preferred_element_type=jnp.float32
            )
            * score_scale
        )
        value_grads = value_grads + jnp.einsum(
            "hqk,qhd->khd",
            probability.astype(jnp.bfloat16),
            grad_block,
            preferred_element_type=jnp.float32,
        )
        return ((key_grads, value_grads), query_grad)

    zero_heads = jnp.zeros((group_rows, local_heads, HEAD), jnp.float32)
    (key_grads, value_grads), query_grads = lax.scan(
        back_block,
        (zero_heads, zero_heads),
        (query_blocks, segment_blocks, place_blocks, att_blocks, log_totals),
    )
    query_grads = query_grads.reshape(group_rows, local_heads, HEAD)
    proj_grad = (
        jnp.stack(
            [
                rotate(query_grads, wave_cos, -wave_sin),
                rotate(key_grads, wave_cos, -wave_sin),
                value_grads,
            ],
            axis=2,
        )
        .reshape(group_rows, 3 * local_heads * HEAD)
        .astype(jnp.bfloat16)
    )
    grad_qkv = contract(normed_one, proj_grad, 0, 0)
    norm_one_grad = contract(proj_grad, qkv_back, 1, 1)
    own_one_grad, own_two_grad = (
        lax.psum_scatter(norm_one_grad, "tensor", scatter_dimension=0, tiled=True),
        lax.psum_scatter(norm_two_grad, "tensor", scatter_dimension=0, tiled=True),
    )
    norm_value, norm_pull = jax.vjp(norms_pair, tokens_f, gain_one, bias_one, gain_two, bias_two)
    row_grad, gain_one_grad, bias_one_grad, gain_two_grad, bias_two_grad = norm_pull(
        (own_one_grad, own_two_grad)
    )
    grad_tokens = grad_out.astype(jnp.float32) + row_grad
    norm_grads = jnp.stack([gain_one_grad, bias_one_grad, gain_two_grad, bias_two_grad], axis=1)
    qkv_parts, up_parts, out_parts, down_parts, norm_parts = (
        lax.all_to_all(grad_qkv[None], "dp", split_axis=1, concat_axis=0, tiled=True),
        lax.all_to_all(grad_up[None], "dp", split_axis=1, concat_axis=0, tiled=True),
        lax.all_to_all(grad_out_t[None], "dp", split_axis=1, concat_axis=0, tiled=True),
        lax.all_to_all(grad_down_t[None], "dp", split_axis=1, concat_axis=0, tiled=True),
        lax.all_to_all(norm_grads[None], "dp", split_axis=1, concat_axis=0, tiled=True),
    )
    qkv_own = jnp.sum(qkv_parts, axis=0)
    up_own = jnp.sum(up_parts, axis=0)
    out_own = jnp.sum(out_parts, axis=0)
    down_own = jnp.sum(down_parts, axis=0)
    norm_own = jnp.sum(norm_parts, axis=0).T
    norm_total = lax.psum(norm_own, "tensor")
    return (
        output,
        grad_tokens,
        norm_total[0],
        norm_total[1],
        norm_total[2],
        norm_total[3],
        qkv_own,
        out_own.T,
        up_own,
        down_own.T,
    )


MESH = pl.DeviceIdType.MESH
FIRST = (0, 32)
SECOND = (32, 16)


def place_of():
    me = lax.axis_index("dp")
    return me // 4, lax.rem(me // 2, 2), lax.rem(me, 2), lax.axis_index("tensor")


def flat(z, x, core):
    return z * 4 + x * 2 + core


def greet(z, x, core, side):
    barrier = pltpu.get_barrier_semaphore()

    def hello(dp, tensor):
        pl.semaphore_signal(barrier, inc=1, device_id=(dp, tensor), device_id_type=MESH)

    hello(flat(z, 1 - x, core), side)
    hello(flat(z, x, 1 - core), side)
    hello(flat(z, x, core), 1 - side)

    @pl.when(z > 0)
    def _():
        hello(flat(z - 1, x, core), side)

    @pl.when(z < 3)
    def _():
        hello(flat(z + 1, x, core), side)

    edge = jnp.where((z == 0) | (z == 3), 1, 0)
    pl.semaphore_wait(barrier, 5 - edge)


class Sender:
    def __init__(self, send_sem):
        self.send_sem = send_sem
        self.count = 0
        self.pending = []

    def send(self, source, target, arrive, dp, tensor, cond, like):
        copy = pltpu.make_async_remote_copy(
            src_ref=source,
            dst_ref=target,
            send_sem=self.send_sem.at[self.count],
            recv_sem=arrive,
            device_id=(dp, tensor),
            device_id_type=MESH,
        )
        self.pending.append((self.count, cond, like))
        self.count += 1
        copy.start()

    def drain(self):
        me, side = lax.axis_index("dp"), lax.axis_index("tensor")
        for index, cond, like in self.pending:

            def finish():
                pltpu.make_async_remote_copy(
                    src_ref=like(),
                    dst_ref=like(),
                    send_sem=self.send_sem.at[index],
                    recv_sem=self.send_sem.at[index],
                    device_id=(me, side),
                    device_id_type=MESH,
                ).wait_send()

            if cond is None:
                finish()
            else:
                pl.when(cond())(finish)


def gather_kernel(shard, tok, cot, full, tok_all, cot_all, send_sem, recv_sem, local_sem):
    z, x, core, side = place_of()
    me = flat(z, x, core)
    greet(z, x, core, side)
    sender = Sender(send_sem)
    ids = {}

    def arrive(*name):
        return recv_sem.at[ids.setdefault(name, len(ids))]

    def part(ref, index, rows):
        return ref.at[index, pl.ds(rows[0], rows[1]), :]

    def shard_part(index, rows, own):
        return shard.at[pl.ds(rows[0], rows[1]), :] if own else part(full, index, rows)

    def move(index, rows, name, dp, tensor, cond, own):
        sender.send(
            shard_part(index, rows, own),
            part(full, index, rows),
            arrive(*name),
            dp,
            tensor,
            cond,
            lambda: part(full, 0, rows),
        )

    def await_part(index, rows, name):
        here = part(full, index, rows)
        pltpu.make_async_remote_copy(
            src_ref=here,
            dst_ref=here,
            send_sem=send_sem.at[0],
            recv_sem=arrive(*name),
            device_id=(me, side),
            device_id_type=MESH,
        ).wait_recv()

    def along(way, near, rows, index, other, cond, own):
        def both():
            inside = z < 3 if way > 0 else z > 0
            return inside if cond is None else inside & cond()

        @pl.when(z < 3 if way > 0 else z > 0)
        def _():
            move(index, rows, ("z", way, near, rows, other), flat(z + way, x, core), side, both, own)

    def across(index, rows, distance, cond, own):
        move(index, rows, ("x", rows, distance), flat(z, 1 - x, core), side, cond, own)

    def sibling(index, rows, name, cond, own):
        move(index, rows, ("c", rows) + name, flat(z, x, 1 - core), side, cond, own)

    half = tok.shape[0]
    mine = pl.ds(side * half, half)
    own_copies = [
        pltpu.make_async_copy(shard, full.at[me], local_sem.at[0]),
        pltpu.make_async_copy(tok, tok_all.at[mine, :], local_sem.at[1]),
        pltpu.make_async_copy(cot, cot_all.at[mine, :], local_sem.at[2]),
    ]
    for way in (1, -1):
        along(way, 1, FIRST, me, 0, None, True)
    across(me, SECOND, 0, None, True)
    across(me, FIRST, 0, None, True)
    for way in (1, -1):
        along(way, 1, SECOND, me, 0, None, True)
    sender.send(tok, tok_all.at[mine, :], arrive("tok"), me, 1 - side, None, lambda: tok)
    sender.send(cot, cot_all.at[mine, :], arrive("cot"), me, 1 - side, None, lambda: cot)
    sibling(me, FIRST, (0, 0), None, True)
    sibling(me, SECOND, (0, 0), None, True)
    for copy in own_copies:
        copy.start()

    other_here = flat(z, 1 - x, core)
    await_part(other_here, SECOND, ("x", SECOND, 0))
    for way in (1, -1):
        along(way, 1, SECOND, other_here, 1, None, False)
    sibling(other_here, SECOND, (0, 1), None, False)

    def from_x(distance):
        index = flat(z + distance, 1 - x, core)
        if distance == 0:
            await_part(index, FIRST, ("x", FIRST, distance))
            sibling(index, FIRST, (distance, 1), None, False)
        else:
            def cond():
                return (z + distance >= 0) & (z + distance <= 3)

            @pl.when(cond())
            def _():
                await_part(index, FIRST, ("x", FIRST, distance))
                sibling(index, FIRST, (distance, 1), cond, False)

    for near in (1, 2, 3):
        for rows, other in ((FIRST, 0), (SECOND, 0), (SECOND, 1)):
            for way in (1, -1):
                def cond(way=way, near=near):
                    return (z - near >= 0) if way > 0 else (z + near <= 3)

                @pl.when(cond())
                def _():
                    index = flat(z - way * near, x if other == 0 else 1 - x, core)
                    await_part(index, rows, ("z", way, near, rows, other))
                    if near < 3:
                        along(way, near + 1, rows, index, other, cond, False)
                    if rows == FIRST:
                        across(index, rows, -way * near, cond, False)
                    sibling(index, rows, (-way * near, other), cond, False)

        if near == 1:
            from_x(0)
        else:
            from_x(near - 1)
            from_x(1 - near)
    from_x(3)
    from_x(-3)

    for distance in range(-3, 4):
        for other in (0, 1):
            for rows in (FIRST, SECOND):

                def take():
                    index = flat(z + distance, x if other == 0 else 1 - x, 1 - core)
                    await_part(index, rows, ("c", rows, distance, other))

                if distance == 0:
                    take()
                else:
                    pl.when((z + distance >= 0) & (z + distance <= 3))(take)
    theirs = pl.ds((1 - side) * half, half)
    for name, ref in (("tok", tok_all), ("cot", cot_all)):
        here = ref.at[theirs, :]
        pltpu.make_async_remote_copy(
            src_ref=here,
            dst_ref=here,
            send_sem=send_sem.at[0],
            recv_sem=arrive(name),
            device_id=(me, side),
            device_id_type=MESH,
        ).wait_recv()
    for copy in own_copies:
        copy.wait()
    sender.drain()


def gather_all(shard, tok, cot):
    rows, width = shard.shape
    vmem = pl.BlockSpec(memory_space=pltpu.VMEM)
    return pl.pallas_call(
        gather_kernel,
        out_shape=(
            jax.ShapeDtypeStruct((16, rows, width), shard.dtype),
            jax.ShapeDtypeStruct((2 * tok.shape[0], tok.shape[1]), tok.dtype),
            jax.ShapeDtypeStruct((2 * cot.shape[0], cot.shape[1]), cot.dtype),
        ),
        in_specs=[vmem] * 3,
        out_specs=(vmem,) * 3,
        scratch_shapes=[
            pltpu.SemaphoreType.DMA((80,)),
            pltpu.SemaphoreType.DMA((80,)),
            pltpu.SemaphoreType.DMA((3,)),
        ],
        compiler_params=pltpu.CompilerParams(
            collective_id=0, has_side_effects=True, vmem_limit_bytes=40 * 1024 * 1024
        ),
        name="gather_all",
    )(shard, tok, cot)


def reduce_kernel(
    parts, to_peer, total, from_peer, sums, from_core, from_x, up, down, last_x, norm_send,
    norm_recv, send_sem, recv_sem
):
    z, x, core, side = place_of()
    me = flat(z, x, core)
    greet(z, x, core, side)
    sender = Sender(send_sem)
    ids = {}
    width = parts.shape[2]
    a_rows, b_rows = pl.ds(*FIRST), pl.ds(*SECOND)

    def arrive(*name):
        return recv_sem.at[ids.setdefault(name, len(ids))]

    def await_at(ref, *name):
        pltpu.make_async_remote_copy(
            src_ref=ref,
            dst_ref=ref,
            send_sem=send_sem.at[0],
            recv_sem=arrive(*name),
            device_id=(me, side),
            device_id_type=MESH,
        ).wait_recv()

    def add(target, left, right, rows):
        @pl.loop(0, rows // 16)
        def _(step):
            at = pl.ds(pl.multiple_of(step * 16, 16), 16)
            target[at, :] = left[at, :] + right[at, :]

    def zq(q):
        return jnp.where(z < 2, q, 3 - q)

    order = [(q, other) for q in (3, 2, 1, 0) for other in (1, 0)]

    def x_of(other):
        return 1 - x if other else x

    for q, other in order:
        sender.send(
            parts.at[flat(zq(q), x_of(other), 1 - core)],
            from_core.at[q * 2 + other],
            arrive("c", q, other),
            flat(z, x, 1 - core),
            side,
            None,
            lambda: parts.at[0],
        )
    sender.send(to_peer, from_peer, arrive("y"), me, 1 - side, None, lambda: to_peer)

    def slot(q, other):
        return q * 2 + other

    def q_of(far):
        return jnp.where(z < 2, z + far, 3 - z - far)

    def buffers(way):
        return up if way > 0 else down

    def chain_send(way, far, kind, block, cond):
        other = 1 if kind == 2 else 0
        rows = a_rows if kind == 0 else b_rows
        buffer = buffers(way)
        base, count = ((0, 32), (32, 16), (48, 16))[kind]
        sender.send(
            sums.at[block, rows, :],
            buffer.at[far - 1, pl.ds(base, count), :],
            arrive("z", way, far - 1, kind),
            flat(z + way, x, core),
            side,
            cond,
            lambda: sums.at[0, rows, :],
        )

    def chain_add(way, far, kind, block):
        rows = a_rows if kind == 0 else b_rows
        base, count = ((0, 32), (32, 16), (48, 16))[kind]
        got = buffers(way).at[far, pl.ds(base, count), :]
        await_at(got, "z", way, far, kind)
        here = sums.at[block, rows, :]
        add(here, here, got, count)

    def take_x(q):
        await_at(from_x.at[q], "x", q)
        here = sums.at[slot(q, 0), a_rows, :]
        add(here, here, from_x.at[q], FIRST[1])

    for q, other in order:
        await_at(from_core.at[q * 2 + other], "c", q, other)
        add(
            sums.at[slot(q, other)],
            parts.at[flat(zq(q), x_of(other), core)],
            from_core.at[q * 2 + other],
            48,
        )
        if other:
            sender.send(
                sums.at[slot(q, 1), a_rows, :],
                from_x.at[q],
                arrive("x", q),
                flat(z, 1 - x, core),
                side,
                None,
                lambda: sums.at[0, a_rows, :],
            )
        else:
            for way in (1, -1):
                if q > 0:
                    def cond(way=way):
                        return (z == 0) if way > 0 else (z == 3)

                    @pl.when(cond())
                    def _():
                        chain_send(way, q, 1, slot(q, 0), cond)
                        chain_send(way, q, 2, slot(q, 1), cond)

            if q < 3:
                take_x(q + 1)
                for way in (1, -1):
                    def cond(way=way):
                        return (z == 0) if way > 0 else (z == 3)

                    @pl.when(cond())
                    def _():
                        chain_send(way, q + 1, 0, slot(q + 1, 0), cond)

    take_x(0)
    for far in (2, 1):
        for kind in (1, 2, 0):
            for way in (1, -1):
                def middle(way=way, far=far):
                    return ((z > 0) & (z + far <= 3)) if way > 0 else ((z < 3) & (z - far >= 0))

                @pl.when(middle())
                def _():
                    q = q_of(way * far)
                    block = q * 2 + (1 if kind == 2 else 0)
                    chain_add(way, far, kind, block)
                    chain_send(way, far, kind, block, middle)

    own_q = jnp.where(z < 2, z, 3 - z)
    for kind in (2, 1, 0):
        block = own_q * 2 + (1 if kind == 2 else 0)
        for way in (1, -1):
            has = (z > 0) if way > 0 else (z < 3)

            @pl.when(has)
            def _():
                chain_add(way, 0, kind, block)

        if kind == 2:
            sender.send(
                sums.at[block, b_rows, :],
                last_x,
                arrive("lx"),
                flat(z, 1 - x, core),
                side,
                None,
                lambda: last_x,
            )
    own = own_q * 2
    norm_at = width - 128

    @pl.loop(0, 2)
    def _(step):
        at = pl.ds(pl.multiple_of(step * 16, 16), 16)
        total[at, :] = sums[own, at, :].astype(jnp.float32)

    await_at(last_x, "lx")
    total[32:48, :] = sums[own, 32:48, :].astype(jnp.float32) + last_x[...].astype(jnp.float32)
    norm_send[...] = total[:, norm_at:]
    sender.send(norm_send, norm_recv, arrive("n"), me, 1 - side, None, lambda: norm_send)
    await_at(norm_recv, "n")
    total[:, norm_at:] = norm_send[...] + norm_recv[...]
    await_at(from_peer, "y")
    sender.drain()


def reduce_all(parts, to_peer):
    _, rows, width = parts.shape
    vmem = pl.BlockSpec(memory_space=pltpu.VMEM)
    low = parts.dtype
    return pl.pallas_call(
        reduce_kernel,
        out_shape=(
            jax.ShapeDtypeStruct((rows, width), jnp.float32),
            jax.ShapeDtypeStruct(to_peer.shape, to_peer.dtype),
        ),
        in_specs=[vmem] * 2,
        out_specs=(vmem,) * 2,
        scratch_shapes=[
            pltpu.VMEM((8, rows, width), low),
            pltpu.VMEM((8, rows, width), low),
            pltpu.VMEM((4, FIRST[1], width), low),
            pltpu.VMEM((3, 64, width), low),
            pltpu.VMEM((3, 64, width), low),
            pltpu.VMEM((SECOND[1], width), low),
            pltpu.VMEM((rows, 128), jnp.float32),
            pltpu.VMEM((rows, 128), jnp.float32),
            pltpu.SemaphoreType.DMA((64,)),
            pltpu.SemaphoreType.DMA((64,)),
        ],
        compiler_params=pltpu.CompilerParams(
            collective_id=1, has_side_effects=True, vmem_limit_bytes=48 * 1024 * 1024
        ),
        name="reduce_all",
    )(parts, to_peer)


def plain_norm(values):
    center = values - jnp.mean(values, axis=-1, keepdims=True)
    spread = jnp.mean(center * center, axis=-1, keepdims=True)
    inverse = lax.rsqrt(spread + norm_eps)
    return center * inverse, inverse


def middle(tok_all, cot_all, weights, norm_float, lengths_row):
    rows = tok_all.shape[0]
    qkv_w, up_w, out_t, down_t = weights
    heads = qkv_w.shape[1] // (3 * HEAD)
    scale = 1.0 / math.sqrt(HEAD)
    gain_one, bias_one, gain_two, bias_two = (norm_float[i][None, :] for i in range(4))
    segment, positions, places = doc_layout(lengths_row, rows)
    wave_cos, wave_sin = rope_tables(positions)
    xhat, _ = plain_norm(tok_all.astype(jnp.float32))
    normed_one = (xhat * gain_one + bias_one).astype(jnp.bfloat16)
    normed_two = (xhat * gain_two + bias_two).astype(jnp.bfloat16)
    projected = contract(normed_one, qkv_w, 1, 0).reshape(rows, heads, 3, HEAD)
    queries = rotate(projected[:, :, 0], wave_cos, wave_sin).astype(jnp.bfloat16)
    keys = rotate(projected[:, :, 1], wave_cos, wave_sin).astype(jnp.bfloat16)
    values = projected[:, :, 2].astype(jnp.bfloat16)
    allowed = (segment[:, None] == segment[None, :]) & (places[:, None] >= places[None, :])
    f32 = jnp.float32
    scores = jnp.einsum("qhd,khd->hqk", queries, keys, preferred_element_type=f32) * scale
    scores = jnp.where(allowed[None], scores, masked_score)
    exponent = jnp.exp(scores - jnp.max(scores, axis=-1, keepdims=True))
    prob = exponent / jnp.sum(exponent, axis=-1, keepdims=True)
    prob_low = prob.astype(jnp.bfloat16)
    attended = jnp.einsum("hqk,khd->qhd", prob_low, values, preferred_element_type=f32)
    attended = attended.astype(jnp.bfloat16).reshape(rows, heads * HEAD)
    hidden = contract(normed_two, up_w, 1, 0)
    cdf = 0.5 * (1.0 + lax.erf(hidden * math.sqrt(0.5)))
    activated = (hidden * cdf).astype(jnp.bfloat16)
    branch = contract(attended, out_t, 1, 1) + contract(activated, down_t, 1, 1)
    slope = cdf + hidden * jnp.exp(-0.5 * hidden * hidden) * (1.0 / math.sqrt(2.0 * math.pi))
    pre_grad = (slope * contract(cot_all, down_t, 1, 0)).astype(jnp.bfloat16)
    att_grad = contract(cot_all, out_t, 1, 0).astype(jnp.bfloat16).reshape(rows, heads, HEAD)
    prob_grad = jnp.einsum("qhd,khd->hqk", att_grad, values, preferred_element_type=f32)
    row_dot = jnp.sum(prob * prob_grad, axis=-1, keepdims=True)
    score_grad = (prob * (prob_grad - row_dot)).astype(jnp.bfloat16)
    query_grad = jnp.einsum("hqk,khd->qhd", score_grad, keys, preferred_element_type=f32) * scale
    key_grad = jnp.einsum("hqk,qhd->khd", score_grad, queries, preferred_element_type=f32) * scale
    value_grad = jnp.einsum("hqk,qhd->khd", prob_low, att_grad, preferred_element_type=f32)
    proj_grad = jnp.stack(
        [
            rotate(query_grad, wave_cos, -wave_sin),
            rotate(key_grad, wave_cos, -wave_sin),
            value_grad,
        ],
        axis=2,
    )
    proj_grad = proj_grad.reshape(rows, 3 * heads * HEAD).astype(jnp.bfloat16)
    norm_one_grad = contract(proj_grad, qkv_w, 1, 1)
    norm_two_grad = contract(pre_grad, up_w, 1, 1)
    norm_sums = jnp.stack(
        [
            jnp.sum(norm_one_grad * xhat, axis=0),
            jnp.sum(norm_one_grad, axis=0),
            jnp.sum(norm_two_grad * xhat, axis=0),
            jnp.sum(norm_two_grad, axis=0),
        ],
        axis=1,
    )
    low = jnp.bfloat16
    grads = jnp.concatenate(
        [
            contract(normed_one, proj_grad, 0, 0).astype(low),
            contract(normed_two, pre_grad, 0, 0).astype(low),
            contract(cot_all, attended, 0, 0).astype(low),
            contract(cot_all, activated, 0, 0).astype(low),
            jnp.pad(norm_sums, ((0, 0), (0, 124))).astype(low),
        ],
        axis=1,
    )
    return grads, branch, norm_one_grad, norm_two_grad


def line_device(
    tokens, ln1_gain, ln1_bias, ln2_gain, ln2_bias, w_qkv, w_out, w_up, w_down, grad_out, lengths
):
    half = tokens.shape[0]
    side = lax.axis_index("tensor")
    norm_params = jnp.stack([ln1_gain, ln1_bias, ln2_gain, ln2_bias], axis=1)
    shard = jnp.concatenate(
        [w_qkv, w_up, w_out.T, w_down.T, jnp.pad(norm_params, ((0, 0), (0, 124)))], axis=1
    )
    cuts = []
    for piece in (w_qkv.shape[1], w_up.shape[1], w_out.shape[0], w_down.shape[0]):
        cuts.append((cuts[-1] if cuts else 0) + piece)
    full, tok_all, cot_all = gather_all(shard, tokens, grad_out)
    full = full.reshape(-1, full.shape[2])
    weights = (
        full[:, : cuts[0]],
        full[:, cuts[0] : cuts[1]],
        full[:, cuts[1] : cuts[2]],
        full[:, cuts[2] : cuts[3]],
    )
    norm_float = full[:, cuts[3] : cuts[3] + 4].astype(jnp.float32).T
    grads, branch, one_grad, two_grad = middle(tok_all, cot_all, weights, norm_float, lengths[0])
    stacked = jnp.stack([branch, one_grad, two_grad], axis=0).reshape(3, 2, half, -1)
    to_peer = lax.dynamic_index_in_dim(stacked, 1 - side, 1, False).astype(jnp.bfloat16)
    own = lax.dynamic_index_in_dim(stacked, side, 1, False)
    total, from_peer = reduce_all(grads.reshape(16, -1, grads.shape[1]), to_peer)
    summed = own + from_peer.astype(jnp.float32)
    tokens_f = tokens.astype(jnp.float32)
    output = (tokens_f + summed[0]).astype(jnp.bfloat16)
    xhat, inverse = plain_norm(tokens_f)
    grad = summed[1] * norm_float[0][None, :] + summed[2] * norm_float[2][None, :]
    row_grad = inverse * (
        grad
        - jnp.mean(grad, axis=-1, keepdims=True)
        - xhat * jnp.mean(grad * xhat, axis=-1, keepdims=True)
    )
    grad_tokens = grad_out.astype(jnp.float32) + row_grad
    norm_total = total[:, cuts[3] : cuts[3] + 4].T
    return (
        output,
        grad_tokens,
        norm_total[0],
        norm_total[1],
        norm_total[2],
        norm_total[3],
        total[:, : cuts[0]],
        total[:, cuts[1] : cuts[2]].T,
        total[:, cuts[0] : cuts[1]],
        total[:, cuts[2] : cuts[3]].T,
    )


def solution(mesh):
    placed = (
        P(("dp", "tensor"), None),
        P("dp"),
        P("dp"),
        P("dp"),
        P("dp"),
        P("dp", "tensor"),
        P("tensor", "dp"),
        P("dp", "tensor"),
        P("tensor", "dp"),
        P(("dp", "tensor"), None),
        P("dp", None),
    )
    body = line_device if mesh.shape["dp"] == 16 and mesh.shape["tensor"] == 2 else per_device
    return jax.shard_map(
        body,
        mesh=mesh,
        in_specs=placed,
        out_specs=(
            P(("dp", "tensor"), None),
            P(("dp", "tensor"), None),
            P("dp"),
            P("dp"),
            P("dp"),
            P("dp"),
            P("dp", "tensor"),
            P("tensor", "dp"),
            P("dp", "tensor"),
            P("tensor", "dp"),
        ),
        check_vma=False,
    )
```

```python
import math

import jax
import jax.numpy as jnp
from jax import lax
from jax.experimental import pallas as pl
from jax.experimental.pallas import tpu as pltpu
from jax.sharding import PartitionSpec as P

HEAD = 64
ROT = 16


norm_eps = 1e-05
masked_score = -1e30


def layer_norm(values, norm_gain, norm_bias):
    center = values - jnp.mean(values, axis=-1, keepdims=True)
    spread = jnp.mean(center * center, axis=-1, keepdims=True)
    return center * lax.rsqrt(spread + norm_eps) * norm_gain + norm_bias


def norms_pair(rows_f, gain_one, bias_one, gain_two, bias_two):
    return (layer_norm(rows_f, gain_one, bias_one), layer_norm(rows_f, gain_two, bias_two))


def doc_layout(lengths_row, row_count):
    seq_ends = jnp.cumsum(lengths_row)
    starts = seq_ends - lengths_row
    places = jnp.arange(row_count, dtype=jnp.int32)
    segment = jnp.sum((places[:, None] >= seq_ends[None, :]).astype(jnp.int32), axis=1)
    chosen = segment[:, None] == jnp.arange(lengths_row.shape[0], dtype=jnp.int32)[None, :]
    seq_first = jnp.sum(jnp.where(chosen, starts[None, :], 0), axis=1)
    return (segment, places - seq_first, places)


def rope_tables(positions):
    frequency = jnp.arange(ROT // 2, dtype=jnp.float32)
    inverse = jnp.exp(frequency * (-2.0 * math.log(10000.0) / ROT))
    angles = positions.astype(jnp.float32)[:, None] * inverse[None, :]
    return (jnp.cos(angles), jnp.sin(angles))


def rotate(vectors, wave_cos, wave_sin):
    half_rot = ROT // 2
    first_half = vectors[..., :half_rot]
    second_half = vectors[..., half_rot:ROT]
    cos_heads = wave_cos[:, None, :]
    sin_heads = wave_sin[:, None, :]
    return jnp.concatenate(
        [
            first_half * cos_heads - second_half * sin_heads,
            second_half * cos_heads + first_half * sin_heads,
            vectors[..., ROT:],
        ],
        axis=-1,
    )


def contract(first_op, second_op, first_dim, second_dim):
    return lax.dot_general(
        first_op,
        second_op,
        (((first_dim,), (second_dim,)), ((), ())),
        preferred_element_type=jnp.float32,
    )


def per_device(
    tokens, ln1_gain, ln1_bias, ln2_gain, ln2_bias, w_qkv, w_out, w_up, w_down, grad_out, lengths
):
    tok_rows = tokens.shape[0]
    group_rows = tok_rows * lax.axis_size("tensor")
    local_heads = w_qkv.shape[1] // (3 * HEAD)
    score_scale = 1.0 / math.sqrt(HEAD)
    norm_params = jnp.stack([ln1_gain, ln1_bias, ln2_gain, ln2_bias], axis=0)
    qkv_full, up_full, out_full, down_full, norm_full = (
        lax.all_gather(w_qkv, "dp", axis=0, tiled=True),
        lax.all_gather(w_up, "dp", axis=0, tiled=True),
        lax.all_gather(w_out, "dp", axis=1, tiled=True),
        lax.all_gather(w_down, "dp", axis=1, tiled=True),
        lax.all_gather(norm_params, "dp", axis=1, tiled=True),
    )
    norm_float = norm_full.astype(jnp.float32)
    gain_one, bias_one, gain_two, bias_two = (
        norm_float[0],
        norm_float[1],
        norm_float[2],
        norm_float[3],
    )
    segment, positions, places = doc_layout(lengths[0], group_rows)
    wave_cos, wave_sin = rope_tables(positions)
    tokens_f = tokens.astype(jnp.float32)
    own_one, own_two = norms_pair(tokens_f, gain_one, bias_one, gain_two, bias_two)
    normed_one, normed_two = (
        lax.all_gather(own_one.astype(jnp.bfloat16), "tensor", axis=0, tiled=True),
        lax.all_gather(own_two.astype(jnp.bfloat16), "tensor", axis=0, tiled=True),
    )
    projected = jnp.dot(normed_one, qkv_full, preferred_element_type=jnp.float32).reshape(
        group_rows, local_heads, 3, HEAD
    )
    queries = rotate(projected[:, :, 0], wave_cos, wave_sin).astype(jnp.bfloat16)
    keys_all = rotate(projected[:, :, 1], wave_cos, wave_sin).astype(jnp.bfloat16)
    values_all = projected[:, :, 2].astype(jnp.bfloat16)
    block_rows = min(512, group_rows)
    block_count = group_rows // block_rows
    query_blocks = queries.reshape(block_count, block_rows, local_heads, HEAD)
    segment_blocks = segment.reshape(block_count, block_rows)
    place_blocks = places.reshape(block_count, block_rows)

    def block_scores(query_block, segment_block, place_block):
        scores = (
            jnp.einsum("qhd,khd->hqk", query_block, keys_all, preferred_element_type=jnp.float32)
            * score_scale
        )
        allowed = (segment_block[:, None] == segment[None, :]) & (
            place_block[:, None] >= places[None, :]
        )
        return jnp.where(allowed[None], scores, masked_score)

    def attend_block(block_items):
        query_block, segment_block, place_block = block_items
        scores = block_scores(query_block, segment_block, place_block)
        row_peak = jnp.max(scores, axis=-1, keepdims=True)
        exponent = jnp.exp(scores - row_peak)
        row_total = jnp.sum(exponent, axis=-1, keepdims=True)
        prob_low = (exponent / row_total).astype(jnp.bfloat16)
        attended_block = jnp.einsum(
            "hqk,khd->qhd", prob_low, values_all, preferred_element_type=jnp.float32
        )
        return (attended_block.astype(jnp.bfloat16), row_peak + jnp.log(row_total))

    attended_blocks, log_totals = lax.map(
        attend_block, (query_blocks, segment_blocks, place_blocks)
    )
    attended = attended_blocks.reshape(group_rows, local_heads * HEAD)
    hidden_pre = jnp.dot(normed_two, up_full, preferred_element_type=jnp.float32)
    activated = jax.nn.gelu(hidden_pre, approximate=False).astype(jnp.bfloat16)
    branch_terms = jnp.dot(attended, out_full, preferred_element_type=jnp.float32) + jnp.dot(
        activated, down_full, preferred_element_type=jnp.float32
    )
    branch_own = lax.psum_scatter(branch_terms, "tensor", scatter_dimension=0, tiled=True)
    output = (tokens_f + branch_own).astype(jnp.bfloat16)
    cotangent = lax.all_gather(grad_out, "tensor", axis=0, tiled=True)
    qkv_back, up_back, out_back, down_back = (
        lax.all_gather(w_qkv, "dp", axis=0, tiled=True),
        lax.all_gather(w_up, "dp", axis=0, tiled=True),
        lax.all_gather(w_out, "dp", axis=1, tiled=True),
        lax.all_gather(w_down, "dp", axis=1, tiled=True),
    )
    act_grad = contract(cotangent, down_back, 1, 1)
    gelu_value, gelu_pull = jax.vjp(
        lambda pre_act: jax.nn.gelu(pre_act, approximate=False), hidden_pre
    )
    pre_grad = gelu_pull(act_grad)[0].astype(jnp.bfloat16)
    grad_down_t = contract(cotangent, activated, 0, 0)
    grad_up = contract(normed_two, pre_grad, 0, 0)
    norm_two_grad = contract(pre_grad, up_back, 1, 1)
    att_grad = contract(cotangent, out_back, 1, 1).astype(jnp.bfloat16)
    grad_out_t = contract(cotangent, attended, 0, 0)
    att_blocks = att_grad.reshape(block_count, block_rows, local_heads, HEAD)

    def back_block(carry, block_items):
        key_grads, value_grads = carry
        query_block, segment_block, place_block, grad_block, log_block = block_items
        scores = block_scores(query_block, segment_block, place_block)
        probability = jnp.exp(scores - log_block)
        prob_grad = jnp.einsum(
            "qhd,khd->hqk", grad_block, values_all, preferred_element_type=jnp.float32
        )
        row_dot = jnp.sum(probability * prob_grad, axis=-1, keepdims=True)
        score_grad = (probability * (prob_grad - row_dot)).astype(jnp.bfloat16)
        query_grad = (
            jnp.einsum("hqk,khd->qhd", score_grad, keys_all, preferred_element_type=jnp.float32)
            * score_scale
        )
        key_grads = (
            key_grads
            + jnp.einsum(
                "hqk,qhd->khd", score_grad, query_block, preferred_element_type=jnp.float32
            )
            * score_scale
        )
        value_grads = value_grads + jnp.einsum(
            "hqk,qhd->khd",
            probability.astype(jnp.bfloat16),
            grad_block,
            preferred_element_type=jnp.float32,
        )
        return ((key_grads, value_grads), query_grad)

    zero_heads = jnp.zeros((group_rows, local_heads, HEAD), jnp.float32)
    (key_grads, value_grads), query_grads = lax.scan(
        back_block,
        (zero_heads, zero_heads),
        (query_blocks, segment_blocks, place_blocks, att_blocks, log_totals),
    )
    query_grads = query_grads.reshape(group_rows, local_heads, HEAD)
    proj_grad = (
        jnp.stack(
            [
                rotate(query_grads, wave_cos, -wave_sin),
                rotate(key_grads, wave_cos, -wave_sin),
                value_grads,
            ],
            axis=2,
        )
        .reshape(group_rows, 3 * local_heads * HEAD)
        .astype(jnp.bfloat16)
    )
    grad_qkv = contract(normed_one, proj_grad, 0, 0)
    norm_one_grad = contract(proj_grad, qkv_back, 1, 1)
    own_one_grad, own_two_grad = (
        lax.psum_scatter(norm_one_grad, "tensor", scatter_dimension=0, tiled=True),
        lax.psum_scatter(norm_two_grad, "tensor", scatter_dimension=0, tiled=True),
    )
    norm_value, norm_pull = jax.vjp(norms_pair, tokens_f, gain_one, bias_one, gain_two, bias_two)
    row_grad, gain_one_grad, bias_one_grad, gain_two_grad, bias_two_grad = norm_pull(
        (own_one_grad, own_two_grad)
    )
    grad_tokens = grad_out.astype(jnp.float32) + row_grad
    norm_grads = jnp.stack([gain_one_grad, bias_one_grad, gain_two_grad, bias_two_grad], axis=1)
    qkv_parts, up_parts, out_parts, down_parts, norm_parts = (
        lax.all_to_all(grad_qkv[None], "dp", split_axis=1, concat_axis=0, tiled=True),
        lax.all_to_all(grad_up[None], "dp", split_axis=1, concat_axis=0, tiled=True),
        lax.all_to_all(grad_out_t[None], "dp", split_axis=1, concat_axis=0, tiled=True),
        lax.all_to_all(grad_down_t[None], "dp", split_axis=1, concat_axis=0, tiled=True),
        lax.all_to_all(norm_grads[None], "dp", split_axis=1, concat_axis=0, tiled=True),
    )
    qkv_own = jnp.sum(qkv_parts, axis=0)
    up_own = jnp.sum(up_parts, axis=0)
    out_own = jnp.sum(out_parts, axis=0)
    down_own = jnp.sum(down_parts, axis=0)
    norm_own = jnp.sum(norm_parts, axis=0).T
    norm_total = lax.psum(norm_own, "tensor")
    return (
        output,
        grad_tokens,
        norm_total[0],
        norm_total[1],
        norm_total[2],
        norm_total[3],
        qkv_own,
        out_own.T,
        up_own,
        down_own.T,
    )


MESH = pl.DeviceIdType.MESH
FIRST = (0, 32)
SECOND = (32, 16)


def place_of():
    me = lax.axis_index("dp")
    return me // 4, lax.rem(me // 2, 2), lax.rem(me, 2), lax.axis_index("tensor")


def flat(z, x, core):
    return z * 4 + x * 2 + core


def greet(z, x, core, side):
    barrier = pltpu.get_barrier_semaphore()

    def hello(dp, tensor):
        pl.semaphore_signal(barrier, inc=1, device_id=(dp, tensor), device_id_type=MESH)

    hello(flat(z, 1 - x, core), side)
    hello(flat(z, x, 1 - core), side)
    hello(flat(z, x, core), 1 - side)

    @pl.when(z > 0)
    def _():
        hello(flat(z - 1, x, core), side)

    @pl.when(z < 3)
    def _():
        hello(flat(z + 1, x, core), side)

    edge = jnp.where((z == 0) | (z == 3), 1, 0)
    pl.semaphore_wait(barrier, 5 - edge)


class Sender:
    def __init__(self, send_sem):
        self.send_sem = send_sem
        self.count = 0
        self.pending = []

    def send(self, source, target, arrive, dp, tensor, cond, like):
        copy = pltpu.make_async_remote_copy(
            src_ref=source,
            dst_ref=target,
            send_sem=self.send_sem.at[self.count],
            recv_sem=arrive,
            device_id=(dp, tensor),
            device_id_type=MESH,
        )
        self.pending.append((self.count, cond, like))
        self.count += 1
        copy.start()

    def drain(self):
        me, side = lax.axis_index("dp"), lax.axis_index("tensor")
        for index, cond, like in self.pending:

            def finish():
                pltpu.make_async_remote_copy(
                    src_ref=like(),
                    dst_ref=like(),
                    send_sem=self.send_sem.at[index],
                    recv_sem=self.send_sem.at[index],
                    device_id=(me, side),
                    device_id_type=MESH,
                ).wait_send()

            if cond is None:
                finish()
            else:
                pl.when(cond())(finish)


def rows_at(ref, index, rows=(0, 48)):
    return ref.at[pl.ds(pl.multiple_of(index * 48 + rows[0], 16), rows[1]), :]


class Arrivals:
    def __init__(self, recv_sem, send_sem, me, side):
        self.recv_sem, self.send_sem, self.me, self.side = recv_sem, send_sem, me, side
        self.ids = {}

    def at(self, *name):
        return self.recv_sem.at[self.ids.setdefault(name, len(self.ids))]

    def wait(self, ref, *name):
        pltpu.make_async_remote_copy(
            src_ref=ref,
            dst_ref=ref,
            send_sem=self.send_sem.at[0],
            recv_sem=self.at(*name),
            device_id=(self.me, self.side),
            device_id_type=MESH,
        ).wait_recv()


class Gather:
    def __init__(self, tag, shard, full, sender, arrivals, local, place):
        self.tag, self.shard, self.full = tag, shard, full
        self.sender, self.arrivals, self.place = sender, arrivals, place
        z, x, core, side = place
        self.copy = pltpu.make_async_copy(shard, rows_at(full, flat(z, x, core)), local)

    def move(self, index, rows, name, dp, cond, own):
        source = self.shard.at[pl.ds(*rows), :] if own else rows_at(self.full, index, rows)
        self.sender.send(
            source,
            rows_at(self.full, index, rows),
            self.arrivals.at(self.tag, *name),
            dp,
            self.place[3],
            cond,
            lambda: rows_at(self.full, 0, rows),
        )

    def take(self, index, rows, name):
        self.arrivals.wait(rows_at(self.full, index, rows), self.tag, *name)

    def along(self, way, near, rows, index, other, cond, own):
        z, x, core, side = self.place

        def both():
            inside = z < 3 if way > 0 else z > 0
            return inside if cond is None else inside & cond()

        @pl.when(z < 3 if way > 0 else z > 0)
        def _():
            name = ("z", way, near, rows, other)
            self.move(index, rows, name, flat(z + way, x, core), both, own)

    def across(self, index, rows, distance, cond, own):
        z, x, core, side = self.place
        self.move(index, rows, ("x", rows, distance), flat(z, 1 - x, core), cond, own)

    def sibling(self, index, rows, name, cond, own):
        z, x, core, side = self.place
        self.move(index, rows, ("c", rows) + name, flat(z, x, 1 - core), cond, own)

    def from_x(self, distance):
        z, x, core, side = self.place

        def cond():
            return (z + distance >= 0) & (z + distance <= 3)

        def pass_on():
            index = flat(z + distance, 1 - x, core)
            self.take(index, FIRST, ("x", FIRST, distance))
            self.sibling(index, FIRST, (distance, 1), cond if distance else None, False)

        pl.when(cond())(pass_on) if distance else pass_on()

    def begin(self):
        z, x, core, side = self.place
        me = flat(z, x, core)
        for way in (1, -1):
            self.along(way, 1, FIRST, me, 0, None, True)
        self.across(me, SECOND, 0, None, True)
        self.across(me, FIRST, 0, None, True)
        for way in (1, -1):
            self.along(way, 1, SECOND, me, 0, None, True)
        self.sibling(me, FIRST, (0, 0), None, True)
        self.sibling(me, SECOND, (0, 0), None, True)
        self.copy.start()

    def hop(self, near):
        z, x, core, side = self.place
        if near == 1:
            here = flat(z, 1 - x, core)
            self.take(here, SECOND, ("x", SECOND, 0))
            for way in (1, -1):
                self.along(way, 1, SECOND, here, 1, None, False)
            self.sibling(here, SECOND, (0, 1), None, False)
        for rows, other in ((FIRST, 0), (SECOND, 0), (SECOND, 1)):
            for way in (1, -1):

                def cond(way=way, near=near):
                    return (z - near >= 0) if way > 0 else (z + near <= 3)

                @pl.when(cond())
                def _():
                    index = flat(z - way * near, 1 - x if other else x, core)
                    self.take(index, rows, ("z", way, near, rows, other))
                    if near < 3:
                        self.along(way, near + 1, rows, index, other, cond, False)
                    if rows == FIRST:
                        self.across(index, rows, -way * near, cond, False)
                    self.sibling(index, rows, (-way * near, other), cond, False)

        if near == 1:
            self.from_x(0)
        else:
            self.from_x(near - 1)
            self.from_x(1 - near)

    def finish(self):
        z, x, core, side = self.place
        self.from_x(3)
        self.from_x(-3)
        for distance in range(-3, 4):
            for other in (0, 1):
                for rows in (FIRST, SECOND):

                    def take():
                        index = flat(z + distance, 1 - x if other else x, 1 - core)
                        self.take(index, rows, ("c", rows, distance, other))

                    if distance == 0:
                        take()
                    else:
                        pl.when((z + distance >= 0) & (z + distance <= 3))(take)
        self.copy.wait()


class Reduce:
    def __init__(self, tag, parts, total, buffers, sender, arrivals, place):
        self.tag, self.parts, self.total = tag, parts, total
        self.sums, self.from_core, self.got_x, self.up, self.down, self.last_x = buffers
        self.sender, self.arrivals, self.place = sender, arrivals, place

    def at(self, *name):
        return self.arrivals.at(self.tag, *name)

    def zq(self, q):
        z = self.place[0]
        return jnp.where(z < 2, q, 3 - q)

    def begin(self):
        z, x, core, side = self.place
        for q in (3, 2, 1, 0):
            for other in (1, 0):
                self.sender.send(
                    rows_at(self.parts, flat(self.zq(q), 1 - x if other else x, 1 - core)),
                    self.from_core.at[q * 2 + other],
                    self.at("c", q, other),
                    flat(z, x, 1 - core),
                    side,
                    None,
                    lambda: rows_at(self.parts, 0),
                )

    def spot(self, kind):
        return ((0, 32), (32, 16), (48, 16))[kind]

    def chain_send(self, way, far, kind, block, cond):
        z, x, core, side = self.place
        rows = FIRST if kind == 0 else SECOND
        buffer = self.up if way > 0 else self.down
        self.sender.send(
            self.sums.at[block, pl.ds(*rows), :],
            buffer.at[far - 1, pl.ds(*self.spot(kind)), :],
            self.at("z", way, far - 1, kind),
            flat(z + way, x, core),
            side,
            cond,
            lambda: self.sums.at[0, pl.ds(*rows), :],
        )

    def add(self, target, left, right, count):
        @pl.loop(0, count // 16)
        def _(step):
            at = pl.ds(pl.multiple_of(step * 16, 16), 16)
            target[at, :] = left[at, :] + right[at, :]

    def chain_add(self, way, far, kind, block):
        rows = FIRST if kind == 0 else SECOND
        got = (self.up if way > 0 else self.down).at[far, pl.ds(*self.spot(kind)), :]
        self.arrivals.wait(got, self.tag, "z", way, far, kind)
        here = self.sums.at[block, pl.ds(*rows), :]
        self.add(here, here, got, rows[1])

    def take_x(self, q):
        self.arrivals.wait(self.got_x.at[q], self.tag, "x", q)
        here = self.sums.at[q * 2, pl.ds(*FIRST), :]
        self.add(here, here, self.got_x.at[q], FIRST[1])

    def edge(self, q, kinds):
        z = self.place[0]
        for way in (1, -1):

            def cond(way=way):
                return (z == 0) if way > 0 else (z == 3)

            @pl.when(cond())
            def _():
                for kind in kinds:
                    self.chain_send(way, q, kind, q * 2 + (1 if kind == 2 else 0), cond)

    def cores(self):
        z, x, core, side = self.place
        for q in (3, 2, 1, 0):
            for other in (1, 0):
                slot = q * 2 + other
                self.arrivals.wait(self.from_core.at[slot], self.tag, "c", q, other)
                mine = rows_at(self.parts, flat(self.zq(q), 1 - x if other else x, core))
                self.add(self.sums.at[slot], mine, self.from_core.at[slot], 48)
                if other:
                    self.sender.send(
                        self.sums.at[slot, pl.ds(*FIRST), :],
                        self.got_x.at[q],
                        self.at("x", q),
                        flat(z, 1 - x, core),
                        side,
                        None,
                        lambda: self.sums.at[0, pl.ds(*FIRST), :],
                    )
            if q > 0:
                self.edge(q, (1, 2))
            if q < 3:
                self.take_x(q + 1)
                self.edge(q + 1, (0,))

    def middle(self, far):
        z = self.place[0]
        if far == 2:
            self.take_x(0)
        for kind in (1, 2, 0):
            for way in (1, -1):

                def cond(way=way, far=far):
                    return ((z > 0) & (z + far <= 3)) if way > 0 else ((z < 3) & (z - far >= 0))

                @pl.when(cond())
                def _():
                    to = z + way * far
                    q = jnp.where(z < 2, to, 3 - to)
                    block = q * 2 + (1 if kind == 2 else 0)
                    self.chain_add(way, far, kind, block)
                    self.chain_send(way, far, kind, block, cond)

    def arrive(self):
        z, x, core, side = self.place
        own_q = jnp.where(z < 2, z, 3 - z)
        for kind in (2, 1, 0):
            block = own_q * 2 + (1 if kind == 2 else 0)
            for way in (1, -1):

                @pl.when((z > 0) if way > 0 else (z < 3))
                def _():
                    self.chain_add(way, 0, kind, block)

            if kind == 2:
                self.sender.send(
                    self.sums.at[block, pl.ds(*SECOND), :],
                    self.last_x,
                    self.at("lx"),
                    flat(z, 1 - x, core),
                    side,
                    None,
                    lambda: self.last_x,
                )
        own = own_q * 2

        @pl.loop(0, 2)
        def _(step):
            at = pl.ds(pl.multiple_of(step * 16, 16), 16)
            self.total[at, :] = self.sums[own, at, :].astype(jnp.float32)

        self.arrivals.wait(self.last_x, self.tag, "lx")
        ours = self.sums[own, 32:48, :].astype(jnp.float32)
        self.total[32:48, :] = ours + self.last_x[...].astype(jnp.float32)


def turn(tile, wave, sign):
    cos, sin_low, sin_high = wave
    ahead = pltpu.roll(tile, 128 - ROT // 2, 1)
    behind = pltpu.roll(tile, ROT // 2, 1)
    return tile * cos[...] + sign * (behind * sin_high[...] - ahead * sin_low[...])


def layer_kernel(*refs):
    (shard0, shard1, shard2, tok, cot, cos, sin_low, sin_high, open_mask) = refs[:9]
    output, grad_tokens, total0, total1, total2 = refs[9:14]
    (
        w0, w1, w2, tok_all, cot_all, cot_t, xhat, params, n1, n2, n1_t, n2_t,
        qs, ks, vs, ags, attended, pg, branch, n1g, n2g, norm_t,
        parts0, parts1, parts2, to_peer, from_peer, norm_send, norm_recv,
    ) = refs[14:43]
    buffers = [refs[43 + 6 * i : 49 + 6 * i] for i in range(3)]
    send_sem, recv_sem, local_sem = refs[61:]
    place = place_of()
    z, x, core, side = place
    me = flat(z, x, core)
    sender = Sender(send_sem)
    arrivals = Arrivals(recv_sem, send_sem, me, side)
    gathers = [
        Gather(("g", i), shard, full, sender, arrivals, local_sem.at[i], place)
        for i, (shard, full) in enumerate(((shard0, w0), (shard1, w1), (shard2, w2)))
    ]
    reduces = [
        Reduce(("r", i), parts, total, buffers[i], sender, arrivals, place)
        for i, (parts, total) in enumerate(
            ((parts0, total0), (parts1, total1), (parts2, total2))
        )
    ]
    low, f32 = jnp.bfloat16, jnp.float32
    half = tok.shape[0]
    mine, theirs = pl.ds(side * half, half), pl.ds((1 - side) * half, half)
    wide = qs.shape[1]
    scale = 1.0 / math.sqrt(HEAD)
    wave = (cos, sin_low, sin_high)

    greet(z, x, core, side)
    gathers[0].begin()
    sender.send(tok, tok_all.at[mine, :], arrivals.at("tok"), me, 1 - side, None, lambda: tok)
    sender.send(cot, cot_all.at[mine, :], arrivals.at("cot"), me, 1 - side, None, lambda: cot)
    tok_all[mine, :] = tok[...]
    cot_all[mine, :] = cot[...]
    arrivals.wait(tok_all.at[theirs, :], "tok")
    arrivals.wait(cot_all.at[theirs, :], "cot")
    xhat[...] = plain_norm(tok_all[...].astype(f32))[0]
    cot_t[...] = cot_all[...].astype(f32).T.astype(low)
    gathers[0].hop(1)
    gathers[1].begin()
    gathers[0].hop(2)
    gathers[0].hop(3)
    gathers[1].hop(1)
    gathers[0].finish()
    gathers[2].begin()

    params[...] = w0[:, 4 * wide :].astype(f32).T
    for at, norm, norm_tr in ((0, n1, n1_t), (2, n2, n2_t)):
        value = xhat[...] * params[at : at + 1, :] + params[at + 1 : at + 2, :]
        norm[...] = value.astype(low)
        norm_tr[...] = value.T.astype(low)
    for at, target in enumerate((qs, ks, vs)):
        tile = contract(n1[...], w0[:, at * wide : (at + 1) * wide], 1, 0)
        for j in range(wide // 128):
            piece = tile[:, j * 128 : (j + 1) * 128]
            if at < 2:
                piece = turn(piece, wave, 1.0)
            target[:, j * 128 : (j + 1) * 128] = piece.astype(low)
    ags[...] = contract(cot_all[...], w0[:, 3 * wide : 4 * wide], 1, 0).astype(low)
    gathers[1].hop(2)

    def pair(j):
        sl = slice(j * 128, (j + 1) * 128)
        q, k, v, ag = qs[:, sl], ks[:, sl], vs[:, sl], ags[:, sl]
        left = lax.broadcasted_iota(jnp.int32, q.shape, 1) < HEAD
        both = []
        for head in (0, 1):
            keep = jnp.where(left, 1.0 - head, 1.0 * head).astype(low)
            scores = contract(q * keep, k, 1, 1) * scale
            scores = jnp.where(open_mask[...] > 0.5, scores, masked_score)
            exponent = jnp.exp(scores - jnp.max(scores, axis=-1, keepdims=True))
            prob = exponent / jnp.sum(exponent, axis=-1, keepdims=True)
            prob_low = prob.astype(low)
            prob_grad = contract(ag * keep, v, 1, 1)
            row_dot = jnp.sum(prob * prob_grad, axis=-1, keepdims=True)
            score_grad = (prob * (prob_grad - row_dot)).astype(low)
            both.append(
                (
                    contract(prob_low, v, 1, 0),
                    contract(score_grad, k, 1, 0) * scale,
                    contract(score_grad, q, 0, 0) * scale,
                    contract(prob_low, ag, 0, 0),
                )
            )
        att, dq, dk, dv = (jnp.where(left, a, b) for a, b in zip(*both))
        attended[:, sl] = att.astype(low)
        pg[:, j * 128 : (j + 1) * 128] = turn(dq, wave, -1.0).astype(low)
        pg[:, wide + j * 128 : wide + (j + 1) * 128] = turn(dk, wave, -1.0).astype(low)
        pg[:, 2 * wide + j * 128 : 2 * wide + (j + 1) * 128] = dv.astype(low)

    pair(0)
    gathers[1].hop(3)
    gathers[2].hop(1)
    pair(1)
    gathers[1].finish()
    pair(2)
    gathers[2].hop(2)
    for at in range(3):
        sl = slice(at * wide, (at + 1) * wide)
        parts0[:, sl] = jnp.dot(n1_t[...], pg[:, sl], preferred_element_type=f32).astype(low)
    parts0[:, 3 * wide :] = jnp.dot(
        cot_t[...], attended[...], preferred_element_type=f32
    ).astype(low)
    reduces[0].begin()
    gathers[2].hop(3)
    n1g[...] = contract(pg[...], w0[:, : 3 * wide], 1, 1)
    branch[...] = contract(attended[...], w0[:, 3 * wide : 4 * wide], 1, 1)
    n2g[...] = jnp.zeros_like(n2g)

    def hidden_part(w, parts):
        size = w.shape[1] // 2

        @pl.loop(0, size // 256)
        def _(step):
            at = pl.ds(pl.multiple_of(step * 256, 256), 256)
            at_down = pl.ds(pl.multiple_of(size + step * 256, 256), 256)
            hidden = contract(n2[...], w[:, at], 1, 0)
            cdf = 0.5 * (1.0 + lax.erf(hidden * math.sqrt(0.5)))
            bell = jnp.exp(-0.5 * hidden * hidden) * (1.0 / math.sqrt(2.0 * math.pi))
            act = (hidden * cdf).astype(low)
            pre = ((cdf + hidden * bell) * contract(cot_all[...], w[:, at_down], 1, 0)).astype(low)
            parts[:, at] = jnp.dot(n2_t[...], pre, preferred_element_type=f32).astype(low)
            parts[:, at_down] = jnp.dot(cot_t[...], act, preferred_element_type=f32).astype(low)
            branch[...] += contract(act, w[:, at_down], 1, 1)
            n2g[...] += contract(pre, w[:, at], 1, 1)

    hidden_part(w1, parts1)
    reduces[0].cores()
    reduces[1].begin()
    gathers[2].finish()
    hidden_part(w2, parts2)
    norm_t[...] = jnp.zeros_like(norm_t)
    for at, grad in ((0, n1g), (2, n2g)):
        norm_t[at : at + 1, :] = jnp.sum(grad[...] * xhat[...], axis=0, keepdims=True)
        norm_t[at + 1 : at + 2, :] = jnp.sum(grad[...], axis=0, keepdims=True)
    parts2[:, w2.shape[1] :] = norm_t[...].T.astype(low)
    reduces[2].begin()
    for at, ref in enumerate((branch, n1g, n2g)):
        to_peer[at] = ref[theirs, :].astype(low)
    sender.send(to_peer, from_peer, arrivals.at("y"), me, 1 - side, None, lambda: to_peer)
    reduces[0].middle(2)
    reduces[1].cores()
    reduces[0].middle(1)
    reduces[0].arrive()
    reduces[1].middle(2)
    reduces[2].cores()
    reduces[1].middle(1)
    reduces[1].arrive()
    reduces[2].middle(2)
    arrivals.wait(from_peer, "y")
    tok_f = tok[...].astype(f32)
    output[...] = (tok_f + (branch[mine, :] + from_peer[0].astype(f32))).astype(low)
    one, two = (ref[mine, :] + from_peer[at].astype(f32) for at, ref in ((1, n1g), (2, n2g)))
    hat, inverse = plain_norm(tok_f)
    grad = one * params[0:1, :] + two * params[2:3, :]
    grad_tokens[...] = cot[...].astype(f32) + inverse * (
        grad
        - jnp.mean(grad, axis=-1, keepdims=True)
        - hat * jnp.mean(grad * hat, axis=-1, keepdims=True)
    )
    reduces[2].middle(1)
    reduces[2].arrive()
    norm_send[...] = total2[:, w2.shape[1] :]
    sender.send(norm_send, norm_recv, arrivals.at("n"), me, 1 - side, None, lambda: norm_send)
    arrivals.wait(norm_recv, "n")
    total2[:, w2.shape[1] :] = norm_send[...] + norm_recv[...]
    sender.drain()


def layer_call(shards, tok, cot, waves, open_mask, heads):
    rows, d = 2 * tok.shape[0], tok.shape[1]
    low, f32 = jnp.bfloat16, jnp.float32
    vmem = pl.BlockSpec(memory_space=pltpu.VMEM)
    wide = heads * HEAD
    widths = [4 * wide, shards[1].shape[1], shards[2].shape[1] + 128]
    out_shape = [jax.ShapeDtypeStruct(tok.shape, low), jax.ShapeDtypeStruct(tok.shape, f32)]
    out_shape += [jax.ShapeDtypeStruct((48, w), f32) for w in widths]
    scratch = [pltpu.VMEM((d, s.shape[1]), low) for s in shards]
    scratch += [pltpu.VMEM((rows, d), low)] * 2
    scratch += [pltpu.VMEM((d, rows), low), pltpu.VMEM((rows, d), f32), pltpu.VMEM((128, d), f32)]
    scratch += [pltpu.VMEM((rows, d), low)] * 2 + [pltpu.VMEM((d, rows), low)] * 2
    scratch += [pltpu.VMEM((rows, wide), low)] * 5
    scratch += [pltpu.VMEM((rows, 3 * wide), low)]
    scratch += [pltpu.VMEM((rows, d), f32)] * 3 + [pltpu.VMEM((128, d), f32)]
    scratch += [pltpu.VMEM((d, w), low) for w in widths]
    scratch += [pltpu.VMEM((3, rows // 2, d), low)] * 2
    scratch += [pltpu.VMEM((48, 128), f32)] * 2
    for w in widths:
        scratch += [pltpu.VMEM((8, 48, w), low)] * 2
        scratch += [pltpu.VMEM((4, FIRST[1], w), low)]
        scratch += [pltpu.VMEM((3, 64, w), low)] * 2
        scratch += [pltpu.VMEM((SECOND[1], w), low)]
    scratch += [pltpu.SemaphoreType.DMA((384,))] * 2 + [pltpu.SemaphoreType.DMA((3,))]
    return pl.pallas_call(
        layer_kernel,
        out_shape=out_shape,
        in_specs=[vmem] * 9,
        out_specs=[vmem] * 5,
        scratch_shapes=scratch,
        compiler_params=pltpu.CompilerParams(
            collective_id=0, has_side_effects=True, vmem_limit_bytes=58 * 1024 * 1024
        ),
        name="layer",
    )(*shards, tok, cot, *waves, open_mask)


def plain_norm(values):
    center = values - jnp.mean(values, axis=-1, keepdims=True)
    spread = jnp.mean(center * center, axis=-1, keepdims=True)
    inverse = lax.rsqrt(spread + norm_eps)
    return center * inverse, inverse


def line_device(
    tokens, ln1_gain, ln1_bias, ln2_gain, ln2_bias, w_qkv, w_out, w_up, w_down, grad_out, lengths
):
    heads = w_qkv.shape[1] // (3 * HEAD)
    own = w_qkv.shape[0]
    wide = heads * HEAD
    split = w_up.shape[1] // 2
    norm_params = jnp.stack([ln1_gain, ln1_bias, ln2_gain, ln2_bias], axis=1)
    qkv = w_qkv.reshape(own, heads, 3, HEAD).transpose(0, 2, 1, 3).reshape(own, 3 * wide)
    down = w_down.T
    shards = (
        jnp.concatenate([qkv, w_out.T, jnp.pad(norm_params, ((0, 0), (0, 124)))], axis=1),
        jnp.concatenate([w_up[:, :split], down[:, :split]], axis=1),
        jnp.concatenate([w_up[:, split:], down[:, split:]], axis=1),
    )
    rows = 2 * tokens.shape[0]
    segment, positions, places = doc_layout(lengths[0], rows)
    wave_cos, wave_sin = rope_tables(positions)
    rest = HEAD - ROT
    none = jnp.zeros_like(wave_sin)
    cos = jnp.concatenate([wave_cos, wave_cos, jnp.ones((rows, rest), jnp.float32)], axis=1)
    blank = jnp.zeros((rows, rest), jnp.float32)
    sin_low = jnp.concatenate([wave_sin, none, blank], axis=1)
    sin_high = jnp.concatenate([none, wave_sin, blank], axis=1)
    waves = [jnp.concatenate([table, table], axis=1) for table in (cos, sin_low, sin_high)]
    allowed = (segment[:, None] == segment[None, :]) & (places[:, None] >= places[None, :])
    output, grad_tokens, total0, total1, total2 = layer_call(
        shards, tokens, grad_out, waves, allowed.astype(jnp.float32), heads
    )
    qkv_grad = total0[:, : 3 * wide].reshape(own, 3, heads, HEAD).transpose(0, 2, 1, 3)
    norm_total = total2[:, 2 * split : 2 * split + 4].T
    return (
        output,
        grad_tokens,
        norm_total[0],
        norm_total[1],
        norm_total[2],
        norm_total[3],
        qkv_grad.reshape(own, 3 * wide),
        total0[:, 3 * wide :].T,
        jnp.concatenate([total1[:, :split], total2[:, :split]], axis=1),
        jnp.concatenate([total1[:, split:], total2[:, split : 2 * split]], axis=1).T,
    )


def solution(mesh):
    placed = (
        P(("dp", "tensor"), None),
        P("dp"),
        P("dp"),
        P("dp"),
        P("dp"),
        P("dp", "tensor"),
        P("tensor", "dp"),
        P("dp", "tensor"),
        P("tensor", "dp"),
        P(("dp", "tensor"), None),
        P("dp", None),
    )
    body = line_device if mesh.shape["dp"] == 16 and mesh.shape["tensor"] == 2 else per_device
    return jax.shard_map(
        body,
        mesh=mesh,
        in_specs=placed,
        out_specs=(
            P(("dp", "tensor"), None),
            P(("dp", "tensor"), None),
            P("dp"),
            P("dp"),
            P("dp"),
            P("dp"),
            P("dp", "tensor"),
            P("tensor", "dp"),
            P("dp", "tensor"),
            P("tensor", "dp"),
        ),
        check_vma=False,
    )
```

```python
import functools
import math

import jax
import jax.numpy as jnp
from jax import lax
from jax.experimental import pallas as pl
from jax.experimental.pallas import tpu as pltpu
from jax.sharding import PartitionSpec as P

HEAD = 64
ROT = 16


norm_eps = 1e-05
masked_score = -1e30


def layer_norm(values, norm_gain, norm_bias):
    center = values - jnp.mean(values, axis=-1, keepdims=True)
    spread = jnp.mean(center * center, axis=-1, keepdims=True)
    return center * lax.rsqrt(spread + norm_eps) * norm_gain + norm_bias


def norms_pair(rows_f, gain_one, bias_one, gain_two, bias_two):
    return (layer_norm(rows_f, gain_one, bias_one), layer_norm(rows_f, gain_two, bias_two))


def doc_layout(lengths_row, row_count):
    seq_ends = jnp.cumsum(lengths_row)
    starts = seq_ends - lengths_row
    places = jnp.arange(row_count, dtype=jnp.int32)
    segment = jnp.sum((places[:, None] >= seq_ends[None, :]).astype(jnp.int32), axis=1)
    chosen = segment[:, None] == jnp.arange(lengths_row.shape[0], dtype=jnp.int32)[None, :]
    seq_first = jnp.sum(jnp.where(chosen, starts[None, :], 0), axis=1)
    return (segment, places - seq_first, places)


def rope_tables(positions):
    frequency = jnp.arange(ROT // 2, dtype=jnp.float32)
    inverse = jnp.exp(frequency * (-2.0 * math.log(10000.0) / ROT))
    angles = positions.astype(jnp.float32)[:, None] * inverse[None, :]
    return (jnp.cos(angles), jnp.sin(angles))


def rotate(vectors, wave_cos, wave_sin):
    half_rot = ROT // 2
    first_half = vectors[..., :half_rot]
    second_half = vectors[..., half_rot:ROT]
    cos_heads = wave_cos[:, None, :]
    sin_heads = wave_sin[:, None, :]
    return jnp.concatenate(
        [
            first_half * cos_heads - second_half * sin_heads,
            second_half * cos_heads + first_half * sin_heads,
            vectors[..., ROT:],
        ],
        axis=-1,
    )


def contract(first_op, second_op, first_dim, second_dim):
    return lax.dot_general(
        first_op,
        second_op,
        (((first_dim,), (second_dim,)), ((), ())),
        preferred_element_type=jnp.float32,
    )


def per_device(
    tokens, ln1_gain, ln1_bias, ln2_gain, ln2_bias, w_qkv, w_out, w_up, w_down, grad_out, lengths
):
    tok_rows = tokens.shape[0]
    group_rows = tok_rows * lax.axis_size("tensor")
    local_heads = w_qkv.shape[1] // (3 * HEAD)
    score_scale = 1.0 / math.sqrt(HEAD)
    norm_params = jnp.stack([ln1_gain, ln1_bias, ln2_gain, ln2_bias], axis=0)
    qkv_full, up_full, out_full, down_full, norm_full = (
        lax.all_gather(w_qkv, "dp", axis=0, tiled=True),
        lax.all_gather(w_up, "dp", axis=0, tiled=True),
        lax.all_gather(w_out, "dp", axis=1, tiled=True),
        lax.all_gather(w_down, "dp", axis=1, tiled=True),
        lax.all_gather(norm_params, "dp", axis=1, tiled=True),
    )
    norm_float = norm_full.astype(jnp.float32)
    gain_one, bias_one, gain_two, bias_two = (
        norm_float[0],
        norm_float[1],
        norm_float[2],
        norm_float[3],
    )
    segment, positions, places = doc_layout(lengths[0], group_rows)
    wave_cos, wave_sin = rope_tables(positions)
    tokens_f = tokens.astype(jnp.float32)
    own_one, own_two = norms_pair(tokens_f, gain_one, bias_one, gain_two, bias_two)
    normed_one, normed_two = (
        lax.all_gather(own_one.astype(jnp.bfloat16), "tensor", axis=0, tiled=True),
        lax.all_gather(own_two.astype(jnp.bfloat16), "tensor", axis=0, tiled=True),
    )
    projected = jnp.dot(normed_one, qkv_full, preferred_element_type=jnp.float32).reshape(
        group_rows, local_heads, 3, HEAD
    )
    queries = rotate(projected[:, :, 0], wave_cos, wave_sin).astype(jnp.bfloat16)
    keys_all = rotate(projected[:, :, 1], wave_cos, wave_sin).astype(jnp.bfloat16)
    values_all = projected[:, :, 2].astype(jnp.bfloat16)
    block_rows = min(512, group_rows)
    block_count = group_rows // block_rows
    query_blocks = queries.reshape(block_count, block_rows, local_heads, HEAD)
    segment_blocks = segment.reshape(block_count, block_rows)
    place_blocks = places.reshape(block_count, block_rows)

    def block_scores(query_block, segment_block, place_block):
        scores = (
            jnp.einsum("qhd,khd->hqk", query_block, keys_all, preferred_element_type=jnp.float32)
            * score_scale
        )
        allowed = (segment_block[:, None] == segment[None, :]) & (
            place_block[:, None] >= places[None, :]
        )
        return jnp.where(allowed[None], scores, masked_score)

    def attend_block(block_items):
        query_block, segment_block, place_block = block_items
        scores = block_scores(query_block, segment_block, place_block)
        row_peak = jnp.max(scores, axis=-1, keepdims=True)
        exponent = jnp.exp(scores - row_peak)
        row_total = jnp.sum(exponent, axis=-1, keepdims=True)
        prob_low = (exponent / row_total).astype(jnp.bfloat16)
        attended_block = jnp.einsum(
            "hqk,khd->qhd", prob_low, values_all, preferred_element_type=jnp.float32
        )
        return (attended_block.astype(jnp.bfloat16), row_peak + jnp.log(row_total))

    attended_blocks, log_totals = lax.map(
        attend_block, (query_blocks, segment_blocks, place_blocks)
    )
    attended = attended_blocks.reshape(group_rows, local_heads * HEAD)
    hidden_pre = jnp.dot(normed_two, up_full, preferred_element_type=jnp.float32)
    activated = jax.nn.gelu(hidden_pre, approximate=False).astype(jnp.bfloat16)
    branch_terms = jnp.dot(attended, out_full, preferred_element_type=jnp.float32) + jnp.dot(
        activated, down_full, preferred_element_type=jnp.float32
    )
    branch_own = lax.psum_scatter(branch_terms, "tensor", scatter_dimension=0, tiled=True)
    output = (tokens_f + branch_own).astype(jnp.bfloat16)
    cotangent = lax.all_gather(grad_out, "tensor", axis=0, tiled=True)
    qkv_back, up_back, out_back, down_back = (
        lax.all_gather(w_qkv, "dp", axis=0, tiled=True),
        lax.all_gather(w_up, "dp", axis=0, tiled=True),
        lax.all_gather(w_out, "dp", axis=1, tiled=True),
        lax.all_gather(w_down, "dp", axis=1, tiled=True),
    )
    act_grad = contract(cotangent, down_back, 1, 1)
    gelu_value, gelu_pull = jax.vjp(
        lambda pre_act: jax.nn.gelu(pre_act, approximate=False), hidden_pre
    )
    pre_grad = gelu_pull(act_grad)[0].astype(jnp.bfloat16)
    grad_down_t = contract(cotangent, activated, 0, 0)
    grad_up = contract(normed_two, pre_grad, 0, 0)
    norm_two_grad = contract(pre_grad, up_back, 1, 1)
    att_grad = contract(cotangent, out_back, 1, 1).astype(jnp.bfloat16)
    grad_out_t = contract(cotangent, attended, 0, 0)
    att_blocks = att_grad.reshape(block_count, block_rows, local_heads, HEAD)

    def back_block(carry, block_items):
        key_grads, value_grads = carry
        query_block, segment_block, place_block, grad_block, log_block = block_items
        scores = block_scores(query_block, segment_block, place_block)
        probability = jnp.exp(scores - log_block)
        prob_grad = jnp.einsum(
            "qhd,khd->hqk", grad_block, values_all, preferred_element_type=jnp.float32
        )
        row_dot = jnp.sum(probability * prob_grad, axis=-1, keepdims=True)
        score_grad = (probability * (prob_grad - row_dot)).astype(jnp.bfloat16)
        query_grad = (
            jnp.einsum("hqk,khd->qhd", score_grad, keys_all, preferred_element_type=jnp.float32)
            * score_scale
        )
        key_grads = (
            key_grads
            + jnp.einsum(
                "hqk,qhd->khd", score_grad, query_block, preferred_element_type=jnp.float32
            )
            * score_scale
        )
        value_grads = value_grads + jnp.einsum(
            "hqk,qhd->khd",
            probability.astype(jnp.bfloat16),
            grad_block,
            preferred_element_type=jnp.float32,
        )
        return ((key_grads, value_grads), query_grad)

    zero_heads = jnp.zeros((group_rows, local_heads, HEAD), jnp.float32)
    (key_grads, value_grads), query_grads = lax.scan(
        back_block,
        (zero_heads, zero_heads),
        (query_blocks, segment_blocks, place_blocks, att_blocks, log_totals),
    )
    query_grads = query_grads.reshape(group_rows, local_heads, HEAD)
    proj_grad = (
        jnp.stack(
            [
                rotate(query_grads, wave_cos, -wave_sin),
                rotate(key_grads, wave_cos, -wave_sin),
                value_grads,
            ],
            axis=2,
        )
        .reshape(group_rows, 3 * local_heads * HEAD)
        .astype(jnp.bfloat16)
    )
    grad_qkv = contract(normed_one, proj_grad, 0, 0)
    norm_one_grad = contract(proj_grad, qkv_back, 1, 1)
    own_one_grad, own_two_grad = (
        lax.psum_scatter(norm_one_grad, "tensor", scatter_dimension=0, tiled=True),
        lax.psum_scatter(norm_two_grad, "tensor", scatter_dimension=0, tiled=True),
    )
    norm_value, norm_pull = jax.vjp(norms_pair, tokens_f, gain_one, bias_one, gain_two, bias_two)
    row_grad, gain_one_grad, bias_one_grad, gain_two_grad, bias_two_grad = norm_pull(
        (own_one_grad, own_two_grad)
    )
    grad_tokens = grad_out.astype(jnp.float32) + row_grad
    norm_grads = jnp.stack([gain_one_grad, bias_one_grad, gain_two_grad, bias_two_grad], axis=1)
    qkv_parts, up_parts, out_parts, down_parts, norm_parts = (
        lax.all_to_all(grad_qkv[None], "dp", split_axis=1, concat_axis=0, tiled=True),
        lax.all_to_all(grad_up[None], "dp", split_axis=1, concat_axis=0, tiled=True),
        lax.all_to_all(grad_out_t[None], "dp", split_axis=1, concat_axis=0, tiled=True),
        lax.all_to_all(grad_down_t[None], "dp", split_axis=1, concat_axis=0, tiled=True),
        lax.all_to_all(norm_grads[None], "dp", split_axis=1, concat_axis=0, tiled=True),
    )
    qkv_own = jnp.sum(qkv_parts, axis=0)
    up_own = jnp.sum(up_parts, axis=0)
    out_own = jnp.sum(out_parts, axis=0)
    down_own = jnp.sum(down_parts, axis=0)
    norm_own = jnp.sum(norm_parts, axis=0).T
    norm_total = lax.psum(norm_own, "tensor")
    return (
        output,
        grad_tokens,
        norm_total[0],
        norm_total[1],
        norm_total[2],
        norm_total[3],
        qkv_own,
        out_own.T,
        up_own,
        down_own.T,
    )


MESH = pl.DeviceIdType.MESH
FIRST = (0, 32)
SECOND = (32, 16)
WHOLE = (0, 48)


def place_of():
    me = lax.axis_index("dp")
    return me // 4, lax.rem(me // 2, 2), lax.rem(me, 2), lax.axis_index("tensor")


def flat(z, x, core):
    return z * 4 + x * 2 + core


def greet(z, x, core, side):
    barrier = pltpu.get_barrier_semaphore()

    def hello(dp, tensor):
        pl.semaphore_signal(barrier, inc=1, device_id=(dp, tensor), device_id_type=MESH)

    hello(flat(z, 1 - x, core), side)
    hello(flat(z, x, 1 - core), side)
    hello(flat(z, x, core), 1 - side)

    @pl.when(z > 0)
    def _():
        hello(flat(z - 1, x, core), side)

    @pl.when(z < 3)
    def _():
        hello(flat(z + 1, x, core), side)

    edge = jnp.where((z == 0) | (z == 3), 1, 0)
    pl.semaphore_wait(barrier, 5 - edge)


class Sender:
    def __init__(self, send_sem):
        self.send_sem = send_sem
        self.count = 0
        self.pending = []

    def send(self, source, target, arrive, dp, tensor, cond, like):
        copy = pltpu.make_async_remote_copy(
            src_ref=source,
            dst_ref=target,
            send_sem=self.send_sem.at[self.count],
            recv_sem=arrive,
            device_id=(dp, tensor),
            device_id_type=MESH,
        )
        self.pending.append((self.count, cond, like))
        self.count += 1
        copy.start()

    def drain(self):
        me, side = lax.axis_index("dp"), lax.axis_index("tensor")
        for index, cond, like in self.pending:

            def finish():
                pltpu.make_async_remote_copy(
                    src_ref=like(),
                    dst_ref=like(),
                    send_sem=self.send_sem.at[index],
                    recv_sem=self.send_sem.at[index],
                    device_id=(me, side),
                    device_id_type=MESH,
                ).wait_send()

            if cond is None:
                finish()
            else:
                pl.when(cond())(finish)


def rows_at(ref, index, rows=(0, 48)):
    return ref.at[pl.ds(pl.multiple_of(index * 48 + rows[0], 16), rows[1]), :]


class Arrivals:
    def __init__(self, recv_sem, send_sem, me, side):
        self.recv_sem, self.send_sem, self.me, self.side = recv_sem, send_sem, me, side
        self.ids = {}

    def at(self, *name):
        return self.recv_sem.at[self.ids.setdefault(name, len(self.ids))]

    def wait(self, ref, *name):
        pltpu.make_async_remote_copy(
            src_ref=ref,
            dst_ref=ref,
            send_sem=self.send_sem.at[0],
            recv_sem=self.at(*name),
            device_id=(self.me, self.side),
            device_id_type=MESH,
        ).wait_recv()


class Gather:
    def __init__(self, tag, shard, full, sender, arrivals, local, place):
        self.tag, self.shard, self.full = tag, shard, full
        self.sender, self.arrivals, self.place = sender, arrivals, place
        z, x, core, side = place
        self.copy = pltpu.make_async_copy(shard, rows_at(full, flat(z, x, core)), local)

    def move(self, index, rows, name, dp, cond, own):
        source = self.shard.at[pl.ds(*rows), :] if own else rows_at(self.full, index, rows)
        self.sender.send(
            source,
            rows_at(self.full, index, rows),
            self.arrivals.at(self.tag, *name),
            dp,
            self.place[3],
            cond,
            lambda: rows_at(self.full, 0, rows),
        )

    def take(self, index, rows, name):
        self.arrivals.wait(rows_at(self.full, index, rows), self.tag, *name)

    def along(self, way, near, rows, index, other, cond, own):
        z, x, core, side = self.place

        def both():
            inside = z < 3 if way > 0 else z > 0
            return inside if cond is None else inside & cond()

        @pl.when(z < 3 if way > 0 else z > 0)
        def _():
            name = ("z", way, near, rows, other)
            self.move(index, rows, name, flat(z + way, x, core), both, own)

    def across(self, index, rows, distance, cond, own):
        z, x, core, side = self.place
        self.move(index, rows, ("x", rows, distance), flat(z, 1 - x, core), cond, own)

    def sibling(self, index, rows, name, cond, own):
        z, x, core, side = self.place
        self.move(index, rows, ("c", rows) + name, flat(z, x, 1 - core), cond, own)

    def from_x(self, distance):
        z, x, core, side = self.place

        def cond():
            return (z + distance >= 0) & (z + distance <= 3)

        def pass_on():
            index = flat(z + distance, 1 - x, core)
            self.take(index, FIRST, ("x", FIRST, distance))
            self.sibling(index, WHOLE, (distance, 1), cond, False)

        pl.when(cond())(pass_on)

    def begin(self):
        z, x, core, side = self.place
        me = flat(z, x, core)
        self.across(me, WHOLE, 0, None, True)
        for way in (1, -1):
            self.along(way, 1, WHOLE, me, 0, None, True)
        self.sibling(me, WHOLE, (0, 0), None, True)
        self.copy.start()

    def hop(self, near):
        z, x, core, side = self.place
        if near == 1:
            here = flat(z, 1 - x, core)
            self.take(here, WHOLE, ("x", WHOLE, 0))
            for way in (1, -1):
                self.along(way, 1, SECOND, here, 1, None, False)
            self.sibling(here, WHOLE, (0, 1), None, False)
        for rows, other in ((WHOLE, 0), (SECOND, 1)):
            for way in (1, -1):

                def cond(way=way, near=near):
                    return (z - near >= 0) if way > 0 else (z + near <= 3)

                @pl.when(cond())
                def _():
                    index = flat(z - way * near, 1 - x if other else x, core)
                    self.take(index, rows, ("z", way, near, rows, other))
                    if near < 3:
                        self.along(way, near + 1, rows, index, other, cond, False)
                    if rows == WHOLE:
                        self.across(index, FIRST, -way * near, cond, False)
                        self.sibling(index, WHOLE, (-way * near, other), cond, False)

        if near > 1:
            self.from_x(near - 1)
            self.from_x(1 - near)

    def finish(self):
        z, x, core, side = self.place
        self.from_x(3)
        self.from_x(-3)
        for distance in range(-3, 4):
            for other in (0, 1):

                def take():
                    index = flat(z + distance, 1 - x if other else x, 1 - core)
                    self.take(index, WHOLE, ("c", WHOLE, distance, other))

                if distance == 0:
                    take()
                else:
                    pl.when((z + distance >= 0) & (z + distance <= 3))(take)
        self.copy.wait()


class Reduce:
    def __init__(self, tag, parts, total, buffers, sender, arrivals, place):
        self.tag, self.parts, self.total = tag, parts, total
        self.sums, self.from_core, self.got_x, self.up, self.down, self.last_x = buffers
        self.sender, self.arrivals, self.place = sender, arrivals, place

    def at(self, *name):
        return self.arrivals.at(self.tag, *name)

    def zq(self, q):
        z = self.place[0]
        return jnp.where(z < 2, q, 3 - q)

    def begin(self):
        z, x, core, side = self.place
        for q in (3, 2, 1, 0):
            for other in (1, 0):
                self.sender.send(
                    rows_at(self.parts, flat(self.zq(q), 1 - x if other else x, 1 - core)),
                    self.from_core.at[q * 2 + other],
                    self.at("c", q, other),
                    flat(z, x, 1 - core),
                    side,
                    None,
                    lambda: rows_at(self.parts, 0),
                )

    def spot(self, kind):
        return (48, 16) if kind else (0, 48)

    def chain_send(self, way, far, kind, block, cond):
        z, x, core, side = self.place
        rows = WHOLE if kind == 0 else SECOND
        buffer = self.up if way > 0 else self.down
        self.sender.send(
            self.sums.at[block, pl.ds(*rows), :],
            buffer.at[far - 1, pl.ds(*self.spot(kind)), :],
            self.at("z", way, far - 1, kind),
            flat(z + way, x, core),
            side,
            cond,
            lambda: self.sums.at[0, pl.ds(*rows), :],
        )

    def add(self, target, left, right, count):
        @pl.loop(0, count // 16)
        def _(step):
            at = pl.ds(pl.multiple_of(step * 16, 16), 16)
            target[at, :] = left[at, :] + right[at, :]

    def chain_add(self, way, far, kind, block):
        rows = WHOLE if kind == 0 else SECOND
        got = (self.up if way > 0 else self.down).at[far, pl.ds(*self.spot(kind)), :]
        self.arrivals.wait(got, self.tag, "z", way, far, kind)
        here = self.sums.at[block, pl.ds(*rows), :]
        self.add(here, here, got, rows[1])

    def take_x(self, q):
        self.arrivals.wait(self.got_x.at[q], self.tag, "x", q)
        here = self.sums.at[q * 2, pl.ds(*FIRST), :]
        self.add(here, here, self.got_x.at[q], FIRST[1])

    def edge(self, q, kinds):
        z = self.place[0]
        for way in (1, -1):

            def cond(way=way):
                return (z == 0) if way > 0 else (z == 3)

            @pl.when(cond())
            def _():
                for kind in kinds:
                    self.chain_send(way, q, kind, q * 2 + (1 if kind == 2 else 0), cond)

    def cores(self):
        z, x, core, side = self.place
        for q in (3, 2, 1, 0):
            for other in (1, 0):
                slot = q * 2 + other
                self.arrivals.wait(self.from_core.at[slot], self.tag, "c", q, other)
                mine = rows_at(self.parts, flat(self.zq(q), 1 - x if other else x, core))
                self.add(self.sums.at[slot], mine, self.from_core.at[slot], 48)
                if other:
                    self.sender.send(
                        self.sums.at[slot, pl.ds(*FIRST), :],
                        self.got_x.at[q],
                        self.at("x", q),
                        flat(z, 1 - x, core),
                        side,
                        None,
                        lambda: self.sums.at[0, pl.ds(*FIRST), :],
                    )
            if q > 0:
                self.edge(q, (2,))
            if q < 3:
                self.take_x(q + 1)
                self.edge(q + 1, (0,))

    def middle(self, far):
        z = self.place[0]
        if far == 2:
            self.take_x(0)
        for kind in (2, 0):
            for way in (1, -1):

                def cond(way=way, far=far):
                    return ((z > 0) & (z + far <= 3)) if way > 0 else ((z < 3) & (z - far >= 0))

                @pl.when(cond())
                def _():
                    to = z + way * far
                    q = jnp.where(z < 2, to, 3 - to)
                    block = q * 2 + (1 if kind == 2 else 0)
                    self.chain_add(way, far, kind, block)
                    self.chain_send(way, far, kind, block, cond)

    def arrive(self):
        z, x, core, side = self.place
        own_q = jnp.where(z < 2, z, 3 - z)
        for kind in (2, 0):
            block = own_q * 2 + (1 if kind == 2 else 0)
            for way in (1, -1):

                @pl.when((z > 0) if way > 0 else (z < 3))
                def _():
                    self.chain_add(way, 0, kind, block)

            if kind == 2:
                self.sender.send(
                    self.sums.at[block, pl.ds(*SECOND), :],
                    self.last_x,
                    self.at("lx"),
                    flat(z, 1 - x, core),
                    side,
                    None,
                    lambda: self.last_x,
                )
        own = own_q * 2

        @pl.loop(0, 2)
        def _(step):
            at = pl.ds(pl.multiple_of(step * 16, 16), 16)
            self.total[at, :] = self.sums[own, at, :].astype(jnp.float32)

        self.arrivals.wait(self.last_x, self.tag, "lx")
        ours = self.sums[own, 32:48, :].astype(jnp.float32)
        self.total[32:48, :] = ours + self.last_x[...].astype(jnp.float32)


def turn(tile, wave, sign):
    cos, sin_low, sin_high = wave
    ahead = pltpu.roll(tile, 128 - ROT // 2, 1)
    behind = pltpu.roll(tile, ROT // 2, 1)
    return tile * cos[...] + sign * (behind * sin_high[...] - ahead * sin_low[...])


ORDER = (
    "g0b ts g1b th",
    "g01 g11 g02 g12",
    "g03 g0f na pr",
    "g13 p0 p1 p2",
    "ag r0b g1f ab",
    "r0c h1 ns r1b",
    "rs r02 r01 r0a",
    "r1c r12 ro r11",
    "r1a no",
)


def layer_kernel(*refs):
    (shard0, shard1, tok, cot, wave_table, open_mask) = refs[:6]
    output, grad_tokens, total0, total1 = refs[6:10]
    (
        w0, w1, tok_all, cot_all, cot_t, xhat, params, n1, n2, n1_t, n2_t,
        qs, ks, vs, ags, attended, pg, branch, n1g, n2g, norm_t,
        parts0, parts1, to_peer, from_peer, norm_send, norm_recv,
    ) = refs[10:37]
    buffers = [refs[37 + 6 * i : 43 + 6 * i] for i in range(2)]
    send_sem, recv_sem, local_sem = refs[49:]
    place = place_of()
    z, x, core, side = place
    me = flat(z, x, core)
    sender = Sender(send_sem)
    arrivals = Arrivals(recv_sem, send_sem, me, side)
    gathers = [
        Gather(("g", i), shard, full, sender, arrivals, local_sem.at[i], place)
        for i, (shard, full) in enumerate(((shard0, w0), (shard1, w1)))
    ]
    reduces = [
        Reduce(("r", i), parts, total, buffers[i], sender, arrivals, place)
        for i, (parts, total) in enumerate(
            ((parts0, total0), (parts1, total1))
        )
    ]
    low, f32 = jnp.bfloat16, jnp.float32
    half = tok.shape[0]
    mine, theirs = pl.ds(side * half, half), pl.ds((1 - side) * half, half)
    wide = qs.shape[1]
    scale = 1.0 / math.sqrt(HEAD)
    wave = [wave_table.at[:, 128 * i : 128 * (i + 1)] for i in range(3)]

    def tokens_sent():
        sender.send(tok, tok_all.at[mine, :], arrivals.at("tok"), me, 1 - side, None, lambda: tok)
        sender.send(cot, cot_all.at[mine, :], arrivals.at("cot"), me, 1 - side, None, lambda: cot)
        tok_all[mine, :] = tok[...]
        cot_all[mine, :] = cot[...]

    def tokens_here():
        arrivals.wait(tok_all.at[theirs, :], "tok")
        arrivals.wait(cot_all.at[theirs, :], "cot")
        xhat[...] = plain_norm(tok_all[...].astype(f32))[0]
        cot_t[...] = cot_all[...].astype(f32).T.astype(low)
        n2g[...] = jnp.zeros_like(n2g)
        norm_t[...] = jnp.zeros_like(norm_t)

    def norms_applied():
        params[...] = w0[:, 4 * wide :].astype(f32).T
        for at, norm, norm_tr in ((0, n1, n1_t), (2, n2, n2_t)):
            value = xhat[...] * params[at : at + 1, :] + params[at + 1 : at + 2, :]
            norm[...] = value.astype(low)
            norm_tr[...] = value.T.astype(low)

    def projections():
        for at, target in enumerate((qs, ks, vs)):
            tile = contract(n1[...], w0[:, at * wide : (at + 1) * wide], 1, 0)
            for j in range(wide // 128):
                piece = tile[:, j * 128 : (j + 1) * 128]
                if at < 2:
                    piece = turn(piece, wave, 1.0)
                target[:, j * 128 : (j + 1) * 128] = piece.astype(low)
        ags[...] = contract(cot_all[...], w0[:, 3 * wide : 4 * wide], 1, 0).astype(low)

    def pair(j):
        sl = slice(j * 128, (j + 1) * 128)
        q, k, v, ag = qs[:, sl], ks[:, sl], vs[:, sl], ags[:, sl]
        left = lax.broadcasted_iota(jnp.int32, q.shape, 1) < HEAD
        both = []
        for head in (0, 1):
            keep = jnp.where(left, 1.0 - head, 1.0 * head).astype(low)
            scores = contract(q * keep, k, 1, 1) * scale
            scores = jnp.where(open_mask[...] > 0.5, scores, masked_score)
            exponent = jnp.exp(scores - jnp.max(scores, axis=-1, keepdims=True))
            prob = exponent / jnp.sum(exponent, axis=-1, keepdims=True)
            prob_low = prob.astype(low)
            prob_grad = contract(ag * keep, v, 1, 1)
            row_dot = jnp.sum(prob * prob_grad, axis=-1, keepdims=True)
            score_grad = (prob * (prob_grad - row_dot)).astype(low)
            both.append(
                (
                    contract(prob_low, v, 1, 0),
                    contract(score_grad, k, 1, 0) * scale,
                    contract(score_grad, q, 0, 0) * scale,
                    contract(prob_low, ag, 0, 0),
                )
            )
        att, dq, dk, dv = (jnp.where(left, a, b) for a, b in zip(*both))
        attended[:, sl] = att.astype(low)
        pg[:, j * 128 : (j + 1) * 128] = turn(dq, wave, -1.0).astype(low)
        pg[:, wide + j * 128 : wide + (j + 1) * 128] = turn(dk, wave, -1.0).astype(low)
        pg[:, 2 * wide + j * 128 : 2 * wide + (j + 1) * 128] = dv.astype(low)

    def attention_grads():
        for at in range(3):
            sl = slice(at * wide, (at + 1) * wide)
            parts0[:, sl] = jnp.dot(n1_t[...], pg[:, sl], preferred_element_type=f32).astype(low)
        parts0[:, 3 * wide :] = jnp.dot(
            cot_t[...], attended[...], preferred_element_type=f32
        ).astype(low)

    def attention_back():
        n1g[...] = contract(pg[...], w0[:, : 3 * wide], 1, 1)
        branch[...] = contract(attended[...], w0[:, 3 * wide : 4 * wide], 1, 1)

    def hidden_part(w, parts):
        size = w.shape[1] // 2

        @pl.loop(0, size // 256)
        def _(step):
            at = pl.ds(pl.multiple_of(step * 256, 256), 256)
            at_down = pl.ds(pl.multiple_of(size + step * 256, 256), 256)
            hidden = contract(n2[...], w[:, at], 1, 0)
            cdf = 0.5 * (1.0 + lax.erf(hidden * math.sqrt(0.5)))
            bell = jnp.exp(-0.5 * hidden * hidden) * (1.0 / math.sqrt(2.0 * math.pi))
            act = (hidden * cdf).astype(low)
            pre = ((cdf + hidden * bell) * contract(cot_all[...], w[:, at_down], 1, 0)).astype(low)
            parts[:, at] = jnp.dot(n2_t[...], pre, preferred_element_type=f32).astype(low)
            parts[:, at_down] = jnp.dot(cot_t[...], act, preferred_element_type=f32).astype(low)
            branch[...] += contract(act, w[:, at_down], 1, 1)
            n2g[...] += contract(pre, w[:, at], 1, 1)

    def norm_sums():
        for at, grad in ((0, n1g), (2, n2g)):
            norm_t[at : at + 1, :] = jnp.sum(grad[...] * xhat[...], axis=0, keepdims=True)
            norm_t[at + 1 : at + 2, :] = jnp.sum(grad[...], axis=0, keepdims=True)
        parts1[:, w1.shape[1] :] = norm_t[...].T.astype(low)

    def rows_sent():
        for at, ref in enumerate((branch, n1g, n2g)):
            to_peer[at] = ref[theirs, :].astype(low)
        sender.send(to_peer, from_peer, arrivals.at("y"), me, 1 - side, None, lambda: to_peer)

    def rows_out():
        arrivals.wait(from_peer, "y")
        tok_f = tok[...].astype(f32)
        output[...] = (tok_f + (branch[mine, :] + from_peer[0].astype(f32))).astype(low)
        one, two = (ref[mine, :] + from_peer[at].astype(f32) for at, ref in ((1, n1g), (2, n2g)))
        hat, inverse = plain_norm(tok_f)
        grad = one * params[0:1, :] + two * params[2:3, :]
        grad_tokens[...] = cot[...].astype(f32) + inverse * (
            grad
            - jnp.mean(grad, axis=-1, keepdims=True)
            - hat * jnp.mean(grad * hat, axis=-1, keepdims=True)
        )

    def norms_out():
        norm_send[...] = total1[:, w1.shape[1] :]
        sender.send(norm_send, norm_recv, arrivals.at("n"), me, 1 - side, None, lambda: norm_send)
        arrivals.wait(norm_recv, "n")
        total1[:, w1.shape[1] :] = norm_send[...] + norm_recv[...]

    steps = {
        "ts": tokens_sent, "th": tokens_here, "na": norms_applied, "pr": projections,
        "ag": attention_grads, "ab": attention_back, "ns": norm_sums, "rs": rows_sent,
        "ro": rows_out, "no": norms_out,
        "h1": lambda: hidden_part(w1, parts1),
    }
    for j in range(wide // 128):
        steps[f"p{j}"] = functools.partial(pair, j)
    for i, item in enumerate(gathers):
        steps[f"g{i}b"], steps[f"g{i}f"] = item.begin, item.finish
        for near in (1, 2, 3):
            steps[f"g{i}{near}"] = functools.partial(item.hop, near)
    for i, item in enumerate(reduces):
        steps[f"r{i}b"], steps[f"r{i}c"], steps[f"r{i}a"] = item.begin, item.cores, item.arrive
        for far in (2, 1):
            steps[f"r{i}{far}"] = functools.partial(item.middle, far)
    greet(z, x, core, side)
    for line in ORDER:
        for name in line.split():
            steps[name]()
    sender.drain()


def layer_call(shards, tok, cot, waves, open_mask, heads):
    rows, d = 2 * tok.shape[0], tok.shape[1]
    low, f32 = jnp.bfloat16, jnp.float32
    vmem = pl.BlockSpec(memory_space=pltpu.VMEM)
    wide = heads * HEAD
    widths = [4 * wide, shards[1].shape[1] + 128]
    out_shape = [jax.ShapeDtypeStruct(tok.shape, low), jax.ShapeDtypeStruct(tok.shape, f32)]
    out_shape += [jax.ShapeDtypeStruct((48, w), f32) for w in widths]
    scratch = [pltpu.VMEM((d, s.shape[1]), low) for s in shards]
    scratch += [pltpu.VMEM((rows, d), low)] * 2
    scratch += [pltpu.VMEM((d, rows), low), pltpu.VMEM((rows, d), f32), pltpu.VMEM((128, d), f32)]
    scratch += [pltpu.VMEM((rows, d), low)] * 2 + [pltpu.VMEM((d, rows), low)] * 2
    scratch += [pltpu.VMEM((rows, wide), low)] * 5
    scratch += [pltpu.VMEM((rows, 3 * wide), low)]
    scratch += [pltpu.VMEM((rows, d), f32)] * 3 + [pltpu.VMEM((128, d), f32)]
    scratch += [pltpu.VMEM((d, w), low) for w in widths]
    scratch += [pltpu.VMEM((3, rows // 2, d), low)] * 2
    scratch += [pltpu.VMEM((48, 128), f32)] * 2
    for w in widths:
        scratch += [pltpu.VMEM((8, 48, w), low)] * 2
        scratch += [pltpu.VMEM((4, FIRST[1], w), low)]
        scratch += [pltpu.VMEM((3, 64, w), low)] * 2
        scratch += [pltpu.VMEM((SECOND[1], w), low)]
    scratch += [pltpu.SemaphoreType.DMA((384,))] * 2 + [pltpu.SemaphoreType.DMA((3,))]
    return pl.pallas_call(
        layer_kernel,
        out_shape=out_shape,
        in_specs=[vmem] * 6,
        out_specs=[vmem] * 4,
        scratch_shapes=scratch,
        compiler_params=pltpu.CompilerParams(
            collective_id=0, has_side_effects=True, vmem_limit_bytes=58 * 1024 * 1024
        ),
        name="layer",
    )(*shards, tok, cot, waves, open_mask)


def plain_norm(values):
    center = values - jnp.mean(values, axis=-1, keepdims=True)
    spread = jnp.mean(center * center, axis=-1, keepdims=True)
    inverse = lax.rsqrt(spread + norm_eps)
    return center * inverse, inverse


def line_device(
    tokens, ln1_gain, ln1_bias, ln2_gain, ln2_bias, w_qkv, w_out, w_up, w_down, grad_out, lengths
):
    heads = w_qkv.shape[1] // (3 * HEAD)
    own = w_qkv.shape[0]
    wide = heads * HEAD
    split = w_up.shape[1]
    norm_params = jnp.stack([ln1_gain, ln1_bias, ln2_gain, ln2_bias], axis=1)
    qkv = w_qkv.reshape(own, heads, 3, HEAD).transpose(0, 2, 1, 3).reshape(own, 3 * wide)
    down = w_down.T
    shards = (
        jnp.concatenate([qkv, w_out.T, jnp.pad(norm_params, ((0, 0), (0, 124)))], axis=1),
        jnp.concatenate([w_up, down], axis=1),
    )
    rows = 2 * tokens.shape[0]
    segment, positions, places = doc_layout(lengths[0], rows)
    wave_cos, wave_sin = rope_tables(positions)
    rest = HEAD - ROT
    none = jnp.zeros_like(wave_sin)
    cos = jnp.concatenate([wave_cos, wave_cos, jnp.ones((rows, rest), jnp.float32)], axis=1)
    blank = jnp.zeros((rows, rest), jnp.float32)
    sin_low = jnp.concatenate([wave_sin, none, blank], axis=1)
    sin_high = jnp.concatenate([none, wave_sin, blank], axis=1)
    waves = jnp.concatenate([cos, cos, sin_low, sin_low, sin_high, sin_high], axis=1)
    allowed = (segment[:, None] == segment[None, :]) & (places[:, None] >= places[None, :])
    output, grad_tokens, total0, total1 = layer_call(
        shards, tokens, grad_out, waves, allowed.astype(jnp.float32), heads
    )
    qkv_grad = total0[:, : 3 * wide].reshape(own, 3, heads, HEAD).transpose(0, 2, 1, 3)
    norm_total = total1[:, 2 * split : 2 * split + 4].T
    return (
        output,
        grad_tokens,
        norm_total[0],
        norm_total[1],
        norm_total[2],
        norm_total[3],
        qkv_grad.reshape(own, 3 * wide),
        total0[:, 3 * wide :].T,
        total1[:, :split],
        total1[:, split : 2 * split].T,
    )


def solution(mesh):
    placed = (
        P(("dp", "tensor"), None),
        P("dp"),
        P("dp"),
        P("dp"),
        P("dp"),
        P("dp", "tensor"),
        P("tensor", "dp"),
        P("dp", "tensor"),
        P("tensor", "dp"),
        P(("dp", "tensor"), None),
        P("dp", None),
    )
    body = line_device if mesh.shape["dp"] == 16 and mesh.shape["tensor"] == 2 else per_device
    return jax.shard_map(
        body,
        mesh=mesh,
        in_specs=placed,
        out_specs=(
            P(("dp", "tensor"), None),
            P(("dp", "tensor"), None),
            P("dp"),
            P("dp"),
            P("dp"),
            P("dp"),
            P("dp", "tensor"),
            P("tensor", "dp"),
            P("dp", "tensor"),
            P("tensor", "dp"),
        ),
        check_vma=False,
    )
```
